32 devices in a mesh: tm: 8 (over z, x), sensor: 4 (over y, core).
Axes of the slice: x: 2, y: 2, z: 4, core: 2. Of those that a mesh axis runs over, the one named last changes fastest.
Arguments:
- observations: bfloat16 [2048, 16384], P('tm', 'sensor'), may hold values from -6 to 6
- obs_list: int32 [2048, 64], P('tm', 'sensor'), may hold values from -1 to 127, as said below
- gain_rows: bfloat16 [16384, 1024], P('sensor'), may hold values from -0.0068359375 to 0.0068359375
- decay: float32 [2048, 1024], P('tm'), may hold values from 0 to 1
- smooth_gain: float32 [2048, 1024], P('tm'), may hold values from 0 to 1
- model_rate: float32 [1024], replicated, may hold values from 0.5 to 1
- first_state: float32 [1024], replicated, may hold values from -6 to 6
Outputs:
- filtered: float32 [2048, 1024], P('tm', 'sensor')
- smoothed: float32 [2048, 1024], P('tm', 'sensor')
The draws below stay inside these ranges and needn't reach their ends.
Inputs may be any that keep to these rules, and one draw needn't show every extreme that they name: `obs_list`: in row t the 16 slots of sensor index j name distinct blocks from j * 32 to (j + 1) * 32 - 1; -1 marks an empty slot; slots of lower sensor indices are emptier.
All inputs are finite; a program needn't handle non-finite values.
Results may differ from the reference program's by a relative error of at most 0.0003.
Values sent between devices are 32-bit elements; how exact they have to be, the bound alone decides.
A program may use at most 64 MiB of HBM per device.

```python
import math
import jax
import jax.numpy as jnp
from jax import lax

MODE_COUNT = 1024
NB_DEV = 32
SLOT_DEV = 16
HOUR_STEPS = 2048
NBLK = 128
N_SENSOR = 4


def factor_law(key, salt, fast_share):
    key = jax.random.fold_in(key, salt)
    random_keys = jax.random.split(key, 6)
    picked = jax.random.uniform(random_keys[0], (MODE_COUNT,)) < fast_share
    slow_rate = jax.random.uniform(random_keys[1], (MODE_COUNT,), minval=0.05, maxval=0.5) * math.log(10.0) / HOUR_STEPS
    fast_rate = jax.random.uniform(random_keys[2], (MODE_COUNT,), minval=1.0 / 50.0, maxval=1.0 / 30.0)
    decay_rate = jnp.where(picked, fast_rate, slow_rate)
    coarse_noise = jax.random.uniform(random_keys[3], (HOUR_STEPS, MODE_COUNT), minval=0.5, maxval=1.6)
    surge_events = jax.random.randint(random_keys[4], (HOUR_STEPS, MODE_COUNT), 0, HOUR_STEPS) < 2
    surge_multiplier = jax.random.uniform(random_keys[5], (HOUR_STEPS, MODE_COUNT), minval=0.5, maxval=0.8)
    entry_value = jnp.exp(-decay_rate[None, :] * coarse_noise) * jnp.where(surge_events, surge_multiplier, 1.0)
    return entry_value.astype(jnp.float32)


def draw_decay(key, part):
    return factor_law(key, 11, 0.35)


def draw_smooth_gain(key, part):
    return factor_law(key, 23, 0.35)


def draw_obs_list(key, part):
    random_keys = jax.random.split(jax.random.fold_in(key, 37), 2)
    sensor_ids = jnp.arange(N_SENSOR, dtype=jnp.int32)
    highest = jnp.minimum(SLOT_DEV, 1 + SLOT_DEV * (sensor_ids + 1) // N_SENSOR)
    counts = jax.random.randint(random_keys[0], (HOUR_STEPS, N_SENSOR), 0, SLOT_DEV + 1)
    counts = jnp.minimum(counts, highest[None, :])
    counts = counts.at[0, N_SENSOR - 1].set(SLOT_DEV)
    scores = jax.random.randint(random_keys[1], (HOUR_STEPS, N_SENSOR, NB_DEV), 0, 2 ** 20) * NB_DEV + jnp.arange(NB_DEV, dtype=jnp.int32)[None, None, :]
    order = jnp.argsort(scores, axis=2, stable=True).astype(jnp.int32)[:, :, :SLOT_DEV]
    global_ids = order + sensor_ids[None, :, None] * NB_DEV
    slot_index = jnp.arange(SLOT_DEV, dtype=jnp.int32)
    global_ids = jnp.where(slot_index[None, None, :] < counts[:, :, None], global_ids, -1)
    return global_ids.reshape(HOUR_STEPS, N_SENSOR * SLOT_DEV).astype(jnp.int32)


def block_levels(rng, extent, shards, smallest, largest):
    factor_of, own = 1.0, jax.random.fold_in(rng, 6)
    for position, shards_of in shards:
        steps = jnp.exp(jax.random.uniform(jax.random.fold_in(own, position), (shards_of,), jnp.float32, smallest / len(shards), largest / len(shards)))
        factor_of = factor_of * jnp.repeat(steps, extent[position] // shards_of).reshape([-1 if axis == position else 1 for axis in range(len(extent))])
    return factor_of


def scatter_about(own_key, extent, scale, reach, cuts=(), kind=jnp.bfloat16):
    array = scale * jax.random.normal(own_key, extent, jnp.float32)
    if cuts:
        array = array * block_levels(own_key, extent, cuts, -0.22, 0.18)
    return jnp.clip(array, -reach, reach).astype(kind)


def setup_inputs(seed: int = 0) -> dict:
    seeds = jax.random.split(jax.random.key(seed), 8)
    observations = scatter_about(seeds[0], (HOUR_STEPS, NBLK * 128), 1.0, 6.0, ((0, 8), (1, 4)))
    obs_list = draw_obs_list(jax.random.fold_in(seeds[7], 71), 0)
    gain_rows = scatter_about(seeds[2], (NBLK * 128, MODE_COUNT), (100 * SLOT_DEV * N_SENSOR * 128) ** -0.5, 0.0068359375, ((0, 4),))
    decay = draw_decay(jax.random.fold_in(seeds[7], 71), 0)
    smooth_gain = draw_smooth_gain(jax.random.fold_in(seeds[7], 71), 0)
    model_rate = jnp.clip(jax.random.uniform(seeds[5], (MODE_COUNT,), jnp.float32, 0.5, 1.0), 0.5, 1.0)
    first_state = scatter_about(seeds[6], (MODE_COUNT,), 1.0, 6.0, (), jnp.float32)
    return {"observations": observations, "obs_list": obs_list, "gain_rows": gain_rows, "decay": decay, "smooth_gain": smooth_gain, "model_rate": model_rate, "first_state": first_state}


def link(earlier, later):
    return (later[0] * earlier[0], later[0] * earlier[1] + later[1])


def reference(observations, obs_list, gain_rows, decay, smooth_gain, model_rate, first_state):
    blocks = jnp.arange(NBLK, dtype=jnp.int32)

    def add_slot(listed, slot_ids):
        return listed + (slot_ids[:, None] == blocks[None, :]).astype(jnp.float32), None

    listed, _ = lax.scan(add_slot, jnp.zeros((HOUR_STEPS, NBLK), jnp.float32), obs_list.T)
    weighted = (observations.reshape(HOUR_STEPS, NBLK, 128) * listed[:, :, None]).reshape(HOUR_STEPS, NBLK * 128).astype(jnp.bfloat16)
    inflow = jnp.dot(weighted, gain_rows, preferred_element_type=jnp.float32)

    def forward(state, pair):
        state = pair[0] * state + pair[1]
        return state, state

    _, filtered = lax.scan(forward, first_state.astype(jnp.float32), (decay, inflow))
    hours = jnp.arange(HOUR_STEPS, dtype=jnp.int32)
    step_gain = jnp.where((hours == HOUR_STEPS - 1)[:, None], jnp.float32(0.0), smooth_gain)
    offset = filtered - (step_gain * model_rate[None, :]) * filtered

    def backward(state, pair):
        state = pair[0] * state + pair[1]
        return state, state

    _, smoothed = lax.scan(backward, jnp.zeros((MODE_COUNT,), jnp.float32), (step_gain, offset), reverse=True)
    return filtered, smoothed
```

```python
import functools
import jax
import jax.numpy as jnp
from jax import lax
from jax.experimental import pallas as pl
from jax.experimental.pallas import tpu as pltpu
from jax.sharding import PartitionSpec as P

LANES = 128
SEGS = 8
CHUNKS = 4
MESH = pl.DeviceIdType.MESH


def shift_rows(value, count, fill):
    rows = lax.broadcasted_iota(jnp.int32, value.shape, 0)
    moved = pltpu.roll(value, count % SEGS, 0)
    inside = (rows >= count) if count > 0 else (rows < SEGS + count)
    return jnp.where(inside, moved, jnp.float32(fill))


def factor_levels(factor, sign):
    levels = []
    for count in (1, 2, 4):
        levels.append(factor)
        factor = factor * shift_rows(factor, sign * count, 1.0)
    return levels, factor


def chain_rows(levels, value, sign):
    for level, count in zip(levels, (1, 2, 4)):
        value = value + level * shift_rows(value, sign * count, 0.0)
    return value


def kernel(
    nt, ny,
    obs, olist, gain, decay, sgain, rate, first,
    filt_out, smooth_out,
    obs_v, list_v, gain_v, dec_v, sg_v, rate_v, first_v,
    csend, crecv, acc, yrecv,
    fm, am, dm, gm, cm, pm, qm, bm,
    early, late, filt_v, smooth_v,
    obs_sem, gain0_sem, gain_sem, list_sem, dec_sem, sg_sem, par_sem,
    cs_sem, cr_sem, ys_sem, yr_sem, es_sem, er_sem, ls_sem, lr_sem, fo_sem, so_sem,
):
    tm = lax.axis_index("tm")
    sensor = lax.axis_index("sensor")
    y = sensor // 2
    core = sensor % 2
    partner = sensor + 1 - 2 * core
    hours, depth = obs_v.shape
    width = gain_v.shape[2]
    halves = width // LANES
    blocks = depth // LANES
    steps = hours // SEGS
    chunk = depth // CHUNKS

    def y_at(k):
        return lax.rem(y + k, ny)

    order = []
    for k in list(range(1, ny)) + [0]:
        order.append(y_at(k) * 2 + 1 - core)
        order.append(y_at(k) * 2 + core)

    def columns(dest):
        return pl.ds(pl.multiple_of(dest * width, LANES), width)

    list_copy = pltpu.make_async_copy(olist, list_v, list_sem)
    list_copy.start()
    obs_copies, gain0_copies = [], []
    for n in range(CHUNKS):
        part = pl.ds(n * chunk, chunk)
        obs_copies.append(pltpu.make_async_copy(obs.at[:, part], obs_v.at[:, part], obs_sem.at[n]))
        gain0_copies.append(
            pltpu.make_async_copy(
                gain.at[part, columns(order[0])], gain_v.at[0, part], gain0_sem.at[n]
            )
        )
        obs_copies[-1].start()
        gain0_copies[-1].start()
    gain_copies = []
    for b in range(1, 2 * ny):
        copy = pltpu.make_async_copy(gain.at[:, columns(order[b])], gain_v.at[b], gain_sem.at[b])
        copy.start()
        gain_copies.append(copy)
    dec_copies, sg_copies = [], []
    for j in range(halves):
        here = pl.ds(pl.multiple_of(sensor * width + j * LANES, LANES), LANES)
        dec_copies.append(pltpu.make_async_copy(decay.at[:, here], dec_v.at[j], dec_sem.at[j]))
        sg_copies.append(pltpu.make_async_copy(sgain.at[:, here], sg_v.at[j], sg_sem.at[j]))
        dec_copies[-1].start()
        sg_copies[-1].start()
    rate_copy = pltpu.make_async_copy(rate, rate_v, par_sem.at[0])
    first_copy = pltpu.make_async_copy(first, first_v, par_sem.at[1])
    rate_copy.start()
    first_copy.start()

    barrier = pltpu.get_barrier_semaphore()
    peers = [(tm, partner)]
    peers += [(tm, y_at(k) * 2 + core) for k in range(1, ny)]
    peers += [(lax.rem(tm + k, nt), sensor) for k in range(1, nt)]
    for peer in peers:
        pl.semaphore_signal(barrier, inc=1, device_id=peer, device_id_type=MESH)

    list_copy.wait()
    place = list_v[...] - sensor * blocks
    valid = (place >= 0) & (place < blocks)
    bit = jnp.where(valid, lax.shift_left(jnp.int32(1), jnp.where(valid, place, 0)), 0)
    bits = jnp.broadcast_to(jnp.sum(bit, axis=1, keepdims=True), (hours, LANES))

    def gate(b, carry):
        part = pl.ds(pl.multiple_of(b * LANES, LANES), LANES)
        listed = (bits & lax.shift_left(jnp.int32(1), b)) != 0
        value = obs_v[:, part].astype(jnp.float32)
        obs_v[:, part] = jnp.where(listed, value, 0.0).astype(jnp.bfloat16)
        return carry

    def put(ref, value):
        for j in range(halves):
            ref[j] = value[:, j * LANES:(j + 1) * LANES]

    total = None
    for n in range(CHUNKS):
        obs_copies[n].wait()
        lax.fori_loop(n * (blocks // CHUNKS), (n + 1) * (blocks // CHUNKS), gate, 0)
        gain0_copies[n].wait()
        part = pl.ds(n * chunk, chunk)
        term = jnp.dot(obs_v[:, part], gain_v[0, part], preferred_element_type=jnp.float32)
        total = term if total is None else total + term

    core_copies, y_copies = [], []
    for n, k in enumerate(list(range(1, ny)) + [0]):
        if n > 0:
            gain_copies[2 * n - 1].wait()
            total = jnp.dot(obs_v[...], gain_v[2 * n], preferred_element_type=jnp.float32)
        put(csend.at[n], total)
        if n == 0:
            pl.semaphore_wait(barrier, len(peers))
        copy = pltpu.make_async_remote_copy(
            csend.at[n], crecv.at[n], cs_sem.at[n], cr_sem.at[n],
            device_id=(tm, partner), device_id_type=MESH,
        )
        copy.start()
        core_copies.append(copy)
        gain_copies[2 * n].wait()
        put(acc.at[n], jnp.dot(obs_v[...], gain_v[2 * n + 1], preferred_element_type=jnp.float32))
        if k == 0:
            break
        copy.wait_recv()
        for j in range(halves):
            acc[n, j] = acc[n, j] + crecv[n, j]
            y_copy = pltpu.make_async_remote_copy(
                acc.at[n, j], yrecv.at[n, j], ys_sem.at[n, j], yr_sem.at[n, j],
                device_id=(tm, y_at(k) * 2 + core), device_id_type=MESH,
            )
            y_copy.start()
            y_copies.append(y_copy)

    rate_copy.wait()
    first_copy.wait()
    row_ids = lax.broadcasted_iota(jnp.int32, (SEGS, LANES), 0)
    last_row = (row_ids == SEGS - 1) & (tm == nt - 1)
    ones = jnp.ones((SEGS, LANES), jnp.float32)
    zeros = jnp.zeros((SEGS, LANES), jnp.float32)
    held = []
    for j in range(halves):
        dec_copies[j].wait()
        sg_copies[j].wait()
        rates = jnp.broadcast_to(rate_v[pl.ds(sensor * halves + j, 1), :], (SEGS, LANES))
        prod = ones
        for i in range(steps):
            d = dec_v[j, pl.ds(i, SEGS, stride=steps), :]
            prod = d * prod
            dm[j, i] = d
            pm[j, i] = prod
        back, linear = ones, zeros
        for i in reversed(range(steps)):
            g = sg_v[j, pl.ds(i, SEGS, stride=steps), :]
            if i == steps - 1:
                g = jnp.where(last_row, 0.0, g)
            c = 1.0 - g * rates
            linear = g * linear + c * pm[j, i]
            back = g * back
            gm[j, i] = g
            cm[j, i] = c
            bm[j, i] = linear
            qm[j, i] = back
        p_levels, p_all = factor_levels(prod, 1)
        q_levels, q_all = factor_levels(back, -1)
        p_before = shift_rows(p_all, 1, 1.0)
        q_after = shift_rows(q_all, -1, 1.0)
        b_all = chain_rows(q_levels, linear * p_before, -1)
        b_after = shift_rows(b_all, -1, 0.0)
        early[tm, j, 0:1] = p_all[SEGS - 1:SEGS]
        early[tm, j, 1:2] = q_all[0:1]
        early[tm, j, 2:3] = b_all[0:1]
        early[tm, j, 3:4] = jnp.zeros((1, LANES), jnp.float32)
        held.append((p_levels, q_levels, p_before, q_after, linear, b_after))
    early_copies = []
    for k in range(1, nt):
        copy = pltpu.make_async_remote_copy(
            early.at[tm], early.at[tm], es_sem.at[k], er_sem.at[k],
            device_id=(lax.rem(tm + k, nt), sensor), device_id_type=MESH,
        )
        copy.start()
        early_copies.append(copy)

    core_copies[-1].wait_recv()
    for j in range(halves):
        acc[ny - 1, j] = acc[ny - 1, j] + crecv[ny - 1, j]

    late_copies, carried = [], []
    for j in range(halves):
        for n in range(ny - 1):
            y_copies[n * halves + j].wait_recv()
        state = zeros
        for i in range(steps):
            rows = pl.ds(i, SEGS, stride=steps)
            inflow = acc[ny - 1, j, rows, :]
            for n in range(ny - 1):
                inflow = inflow + yrecv[n, j, rows, :]
            state = dm[j, i] * state + inflow
            fm[j, i] = state
        back = zeros
        for i in reversed(range(steps)):
            back = gm[j, i] * back + cm[j, i] * fm[j, i]
            am[j, i] = back
        p_levels, q_levels, p_before, q_after, linear, b_after = held[j]
        f_all = chain_rows(p_levels, state, 1)
        f_before = shift_rows(f_all, 1, 0.0)
        a_all = chain_rows(q_levels, back + linear * f_before, -1)
        a_after = shift_rows(a_all, -1, 0.0)
        late[j, tm, 0:1] = f_all[SEGS - 1:SEGS]
        late[j, tm, 1:2] = a_all[0:1]
        carried.append((f_before, a_after))
        for k in range(1, nt):
            copy = pltpu.make_async_remote_copy(
                late.at[j, tm], late.at[j, tm], ls_sem.at[j, k], lr_sem.at[j, k],
                device_id=(lax.rem(tm + k, nt), sensor), device_id_type=MESH,
            )
            copy.start()
            late_copies.append(copy)

    out_copies = []
    for j in range(halves):
        if j == 0:
            for copy in early_copies:
                copy.wait_recv()
        for k in range(1, nt):
            late_copies[j * (nt - 1) + k - 1].wait_recv()
        entry = first_v[pl.ds(sensor * halves + j, 1), :]
        entries, mine = [], entry
        for t in range(nt):
            mine = jnp.where(tm == t, entry, mine)
            entries.append(entry)
            entry = early[t, j, 0:1] * entry + late[j, t, 0:1]
        after = jnp.zeros((1, LANES), jnp.float32)
        mine_after = after
        for t in reversed(range(nt)):
            mine_after = jnp.where(tm == t, after, mine_after)
            after = early[t, j, 1:2] * after + (late[j, t, 1:2] + early[t, j, 2:3] * entries[t])
        _, _, p_before, q_after, _, b_after = held[j]
        f_before, a_after = carried[j]
        seg_entry = p_before * mine + f_before
        seg_after = q_after * mine_after + (a_after + b_after * mine)
        for i in range(steps):
            rows = pl.ds(i, SEGS, stride=steps)
            filt_v[j, rows, :] = fm[j, i] + pm[j, i] * seg_entry
            smooth_v[j, rows, :] = am[j, i] + bm[j, i] * seg_entry + qm[j, i] * seg_after
        here = pl.ds(j * LANES, LANES)
        for src, dst, sem in ((filt_v, filt_out, fo_sem), (smooth_v, smooth_out, so_sem)):
            copy = pltpu.make_async_copy(src.at[j], dst.at[:, here], sem.at[j])
            copy.start()
            out_copies.append(copy)

    for copy in core_copies + y_copies + early_copies + late_copies:
        copy.wait_send()
    for copy in out_copies:
        copy.wait()


def per_device(nt, ns, observations, obs_list, gain_rows, decay, smooth_gain, model_rate, first_state):
    ny = ns // 2
    hours, depth = observations.shape
    modes = gain_rows.shape[1]
    width = modes // ns
    halves = width // LANES
    steps = hours // SEGS
    f32 = jnp.float32
    dma = pltpu.SemaphoreType.DMA
    any_space = pl.BlockSpec(memory_space=pl.ANY)
    tiles = pltpu.VMEM((halves, steps, SEGS, LANES), f32)
    plane = pltpu.VMEM((halves, hours, LANES), f32)
    params = pltpu.VMEM((modes // LANES, LANES), f32)
    out = jax.ShapeDtypeStruct((hours, width), f32)
    return pl.pallas_call(
        functools.partial(kernel, nt, ny),
        out_shape=(out, out),
        in_specs=[any_space] * 7,
        out_specs=(any_space, any_space),
        scratch_shapes=[
            pltpu.VMEM((hours, depth), jnp.bfloat16),
            pltpu.VMEM(obs_list.shape, jnp.int32),
            pltpu.VMEM((ns, depth, width), jnp.bfloat16),
            plane, plane, params, params,
            pltpu.VMEM((ny, halves, hours, LANES), f32),
            pltpu.VMEM((ny, halves, hours, LANES), f32),
            pltpu.VMEM((ny, halves, hours, LANES), f32),
            pltpu.VMEM((max(ny - 1, 1), halves, hours, LANES), f32),
            tiles, tiles, tiles, tiles, tiles, tiles, tiles, tiles,
            pltpu.VMEM((nt, halves, 4, LANES), f32),
            pltpu.VMEM((halves, nt, 2, LANES), f32),
            plane, plane,
            dma((CHUNKS,)), dma((CHUNKS,)), dma((ns,)), dma, dma((halves,)), dma((halves,)), dma((2,)),
            dma((ny,)), dma((ny,)), dma((ny, halves)), dma((ny, halves)),
            dma((nt,)), dma((nt,)), dma((halves, nt)), dma((halves, nt)), dma((halves,)), dma((halves,)),
        ],
        compiler_params=pltpu.CompilerParams(
            collective_id=0, has_side_effects=True, vmem_limit_bytes=56 * 1024 * 1024
        ),
        cost_estimate=pl.CostEstimate(
            flops=2 * hours * depth * modes, bytes_accessed=2 * depth * (hours + modes), transcendentals=0
        ),
    )(
        observations, obs_list, gain_rows, decay, smooth_gain,
        model_rate.reshape(modes // LANES, LANES), first_state.reshape(modes // LANES, LANES),
    )


def solution(mesh):
    nt, ns = mesh.shape["tm"], mesh.shape["sensor"]
    in_specs = (
        P("tm", "sensor"),
        P("tm", "sensor"),
        P("sensor", None),
        P("tm", None),
        P("tm", None),
        P(),
        P(),
    )
    out_specs = (P("tm", "sensor"), P("tm", "sensor"))
    return jax.shard_map(
        functools.partial(per_device, nt, ns),
        mesh=mesh, in_specs=in_specs, out_specs=out_specs, check_vma=False,
    )
```

```python
import functools
import jax
import jax.numpy as jnp
from jax import lax
from jax.experimental import pallas as pl
from jax.experimental.pallas import tpu as pltpu
from jax.sharding import PartitionSpec as P

LANES = 128
SEGS = 8
CHUNKS = 4
MESH = pl.DeviceIdType.MESH


def shift_rows(value, count, fill):
    rows = lax.broadcasted_iota(jnp.int32, value.shape, 0)
    moved = pltpu.roll(value, count % SEGS, 0)
    inside = (rows >= count) if count > 0 else (rows < SEGS + count)
    return jnp.where(inside, moved, jnp.float32(fill))


def factor_levels(factor, sign):
    levels = []
    for count in (1, 2, 4):
        levels.append(factor)
        factor = factor * shift_rows(factor, sign * count, 1.0)
    return levels, factor


def chain_rows(levels, value, sign):
    for level, count in zip(levels, (1, 2, 4)):
        value = value + level * shift_rows(value, sign * count, 0.0)
    return value


def kernel(
    nt, ny,
    obs, olist, gain, decay, sgain, rate, first,
    filt_out, smooth_out,
    obs_v, list_v, gain_v, dec_v, sg_v, rate_v, first_v,
    csend, crecv, acc, yrecv,
    fm, am, dm, gm, cm, pm, qm, bm,
    early, late, filt_v, smooth_v,
    obs_sem, gain0_sem, gain_sem, list_sem, dec_sem, sg_sem, par_sem,
    cs_sem, cr_sem, ys_sem, yr_sem, es_sem, er_sem, ls_sem, lr_sem,
):
    tm = lax.axis_index("tm")
    sensor = lax.axis_index("sensor")
    y = sensor // 2
    core = sensor % 2
    partner = sensor + 1 - 2 * core
    hours, depth = obs_v.shape
    width = gain_v.shape[2]
    halves = width // LANES
    blocks = depth // LANES
    steps = hours // SEGS
    chunk = depth // CHUNKS

    def y_at(k):
        return lax.rem(y + k, ny)

    order = []
    for k in list(range(1, ny)) + [0]:
        order.append(y_at(k) * 2 + 1 - core)
        order.append(y_at(k) * 2 + core)

    def columns(dest):
        return pl.ds(pl.multiple_of(dest * width, LANES), width)

    list_copy = pltpu.make_async_copy(olist, list_v, list_sem)
    list_copy.start()
    obs_copies, gain0_copies = [], []
    for n in range(CHUNKS):
        part = pl.ds(n * chunk, chunk)
        obs_copies.append(pltpu.make_async_copy(obs.at[:, part], obs_v.at[:, part], obs_sem.at[n]))
        gain0_copies.append(
            pltpu.make_async_copy(
                gain.at[part, columns(order[0])], gain_v.at[0, part], gain0_sem.at[n]
            )
        )
        obs_copies[-1].start()
        gain0_copies[-1].start()
    gain_copies = []
    for b in range(1, 2 * ny):
        gain_copies.append(
            pltpu.make_async_copy(gain.at[:, columns(order[b])], gain_v.at[b], gain_sem.at[b])
        )
    dec_copies, sg_copies = [], []
    for j in range(halves):
        here = pl.ds(pl.multiple_of(sensor * width + j * LANES, LANES), LANES)
        dec_copies.append(pltpu.make_async_copy(decay.at[:, here], dec_v.at[j], dec_sem.at[j]))
        sg_copies.append(pltpu.make_async_copy(sgain.at[:, here], sg_v.at[j], sg_sem.at[j]))
    rate_copy = pltpu.make_async_copy(rate, rate_v, par_sem.at[0])
    first_copy = pltpu.make_async_copy(first, first_v, par_sem.at[1])
    barrier = pltpu.get_barrier_semaphore()
    peers = [(tm, partner)]
    peers += [(tm, y_at(k) * 2 + core) for k in range(1, ny)]
    peers += [(lax.rem(tm + k, nt), sensor) for k in range(1, nt)]
    for peer in peers:
        pl.semaphore_signal(barrier, inc=1, device_id=peer, device_id_type=MESH)

    list_copy.wait()
    place = list_v[...] - sensor * blocks
    valid = (place >= 0) & (place < blocks)
    bit = jnp.where(valid, lax.shift_left(jnp.int32(1), jnp.where(valid, place, 0)), 0)
    flat = jnp.broadcast_to(jnp.sum(bit, axis=0, keepdims=True), (LANES, hours))
    bits = jnp.transpose(flat)

    def gate(b, carry):
        part = pl.ds(pl.multiple_of(b * LANES, LANES), LANES)
        listed = (bits & lax.shift_left(jnp.int32(1), b)) != 0
        value = obs_v[:, part].astype(jnp.float32)
        obs_v[:, part] = jnp.where(listed, value, 0.0).astype(jnp.bfloat16)
        return carry

    def put(ref, value):
        for j in range(halves):
            ref[j] = value[:, j * LANES:(j + 1) * LANES]

    total = None
    for n in range(CHUNKS):
        obs_copies[n].wait()
        lax.fori_loop(n * (blocks // CHUNKS), (n + 1) * (blocks // CHUNKS), gate, 0)
        gain0_copies[n].wait()
        if n == CHUNKS // 2 - 1:
            gain_copies[0].start()
        part = pl.ds(n * chunk, chunk)
        term = jnp.dot(obs_v[:, part], gain_v[0, part], preferred_element_type=jnp.float32)
        total = term if total is None else total + term

    for copy in gain_copies[1:] + dec_copies + sg_copies + [rate_copy, first_copy]:
        copy.start()

    core_copies, y_copies = [], []
    for n, k in enumerate(list(range(1, ny)) + [0]):
        if n > 0:
            gain_copies[2 * n - 1].wait()
            total = jnp.dot(obs_v[...], gain_v[2 * n], preferred_element_type=jnp.float32)
        put(csend.at[n], total)
        if n == 0:
            pl.semaphore_wait(barrier, len(peers))
        for j in range(halves):
            copy = pltpu.make_async_remote_copy(
                csend.at[n, j], crecv.at[n, j], cs_sem.at[n, j], cr_sem.at[n, j],
                device_id=(tm, partner), device_id_type=MESH,
            )
            copy.start()
            core_copies.append(copy)
        gain_copies[2 * n].wait()
        put(acc.at[n], jnp.dot(obs_v[...], gain_v[2 * n + 1], preferred_element_type=jnp.float32))
        if k == 0:
            break
        for j in range(halves):
            core_copies[n * halves + j].wait_recv()
            acc[n, j] = acc[n, j] + crecv[n, j]
            y_copy = pltpu.make_async_remote_copy(
                acc.at[n, j], yrecv.at[n, j], ys_sem.at[n, j], yr_sem.at[n, j],
                device_id=(tm, y_at(k) * 2 + core), device_id_type=MESH,
            )
            y_copy.start()
            y_copies.append(y_copy)

    rate_copy.wait()
    first_copy.wait()
    row_ids = lax.broadcasted_iota(jnp.int32, (SEGS, LANES), 0)
    last_row = (row_ids == SEGS - 1) & (tm == nt - 1)
    ones = jnp.ones((SEGS, LANES), jnp.float32)
    zeros = jnp.zeros((SEGS, LANES), jnp.float32)
    held = []
    for j in range(halves):
        dec_copies[j].wait()
        sg_copies[j].wait()
        rates = jnp.broadcast_to(rate_v[pl.ds(sensor * halves + j, 1), :], (SEGS, LANES))
        prod = ones
        for i in range(steps):
            d = dec_v[j, pl.ds(i, SEGS, stride=steps), :]
            prod = d * prod
            dm[j, i] = d
            pm[j, i] = prod
        back, linear = ones, zeros
        for i in reversed(range(steps)):
            g = sg_v[j, pl.ds(i, SEGS, stride=steps), :]
            if i == steps - 1:
                g = jnp.where(last_row, 0.0, g)
            c = 1.0 - g * rates
            linear = g * linear + c * pm[j, i]
            back = g * back
            gm[j, i] = g
            cm[j, i] = c
            bm[j, i] = linear
            qm[j, i] = back
        p_levels, p_all = factor_levels(prod, 1)
        q_levels, q_all = factor_levels(back, -1)
        p_before = shift_rows(p_all, 1, 1.0)
        q_after = shift_rows(q_all, -1, 1.0)
        b_all = chain_rows(q_levels, linear * p_before, -1)
        b_after = shift_rows(b_all, -1, 0.0)
        early[tm, j, 0:1] = p_all[SEGS - 1:SEGS]
        early[tm, j, 1:2] = q_all[0:1]
        early[tm, j, 2:3] = b_all[0:1]
        early[tm, j, 3:4] = jnp.zeros((1, LANES), jnp.float32)
        held.append((p_levels, q_levels, p_before, q_after, linear, b_after))
    early_copies = []
    for k in range(1, nt):
        copy = pltpu.make_async_remote_copy(
            early.at[tm], early.at[tm], es_sem.at[k], er_sem.at[k],
            device_id=(lax.rem(tm + k, nt), sensor), device_id_type=MESH,
        )
        copy.start()
        early_copies.append(copy)

    for j in range(halves):
        core_copies[(ny - 1) * halves + j].wait_recv()
        acc[ny - 1, j] = acc[ny - 1, j] + crecv[ny - 1, j]

    late_copies, carried = [], []
    for j in range(halves):
        for n in range(ny - 1):
            y_copies[n * halves + j].wait_recv()
        state = zeros
        for i in range(steps):
            rows = pl.ds(i, SEGS, stride=steps)
            inflow = acc[ny - 1, j, rows, :]
            for n in range(ny - 1):
                inflow = inflow + yrecv[n, j, rows, :]
            state = dm[j, i] * state + inflow
            fm[j, i] = state
        back = zeros
        for i in reversed(range(steps)):
            back = gm[j, i] * back + cm[j, i] * fm[j, i]
            am[j, i] = back
        p_levels, q_levels, p_before, q_after, linear, b_after = held[j]
        f_all = chain_rows(p_levels, state, 1)
        f_before = shift_rows(f_all, 1, 0.0)
        a_all = chain_rows(q_levels, back + linear * f_before, -1)
        a_after = shift_rows(a_all, -1, 0.0)
        late[j, tm, 0:1] = f_all[SEGS - 1:SEGS]
        late[j, tm, 1:2] = a_all[0:1]
        carried.append((f_before, a_after))
        for k in range(1, nt):
            copy = pltpu.make_async_remote_copy(
                late.at[j, tm], late.at[j, tm], ls_sem.at[j, k], lr_sem.at[j, k],
                device_id=(lax.rem(tm + k, nt), sensor), device_id_type=MESH,
            )
            copy.start()
            late_copies.append(copy)

    for j in range(halves):
        if j == 0:
            for copy in early_copies:
                copy.wait_recv()
        for k in range(1, nt):
            late_copies[j * (nt - 1) + k - 1].wait_recv()
        entry = first_v[pl.ds(sensor * halves + j, 1), :]
        entries, mine = [], entry
        for t in range(nt):
            mine = jnp.where(tm == t, entry, mine)
            entries.append(entry)
            entry = early[t, j, 0:1] * entry + late[j, t, 0:1]
        after = jnp.zeros((1, LANES), jnp.float32)
        mine_after = after
        for t in reversed(range(nt)):
            mine_after = jnp.where(tm == t, after, mine_after)
            after = early[t, j, 1:2] * after + (late[j, t, 1:2] + early[t, j, 2:3] * entries[t])
        _, _, p_before, q_after, _, b_after = held[j]
        f_before, a_after = carried[j]
        seg_entry = p_before * mine + f_before
        seg_after = q_after * mine_after + (a_after + b_after * mine)
        for i in range(steps):
            rows = pl.ds(i, SEGS, stride=steps)
            filt_v[j, rows, :] = fm[j, i] + pm[j, i] * seg_entry
            smooth_v[j, rows, :] = am[j, i] + bm[j, i] * seg_entry + qm[j, i] * seg_after
        filt_out[:, j * LANES:(j + 1) * LANES] = filt_v[j]
        smooth_out[:, j * LANES:(j + 1) * LANES] = smooth_v[j]

    for copy in core_copies + y_copies + early_copies + late_copies:
        copy.wait_send()


def per_device(nt, ns, observations, obs_list, gain_rows, decay, smooth_gain, model_rate, first_state):
    ny = ns // 2
    hours, depth = observations.shape
    modes = gain_rows.shape[1]
    width = modes // ns
    halves = width // LANES
    steps = hours // SEGS
    f32 = jnp.float32
    dma = pltpu.SemaphoreType.DMA
    any_space = pl.BlockSpec(memory_space=pl.ANY)
    tiles = pltpu.VMEM((halves, steps, SEGS, LANES), f32)
    plane = pltpu.VMEM((halves, hours, LANES), f32)
    params = pltpu.VMEM((modes // LANES, LANES), f32)
    out = pltpu.VMEM((hours, width), f32)
    vmem_space = pl.BlockSpec(memory_space=pltpu.VMEM)
    return pl.pallas_call(
        functools.partial(kernel, nt, ny),
        out_shape=(out, out),
        in_specs=[any_space] * 7,
        out_specs=(vmem_space, vmem_space),
        scratch_shapes=[
            pltpu.VMEM((hours, depth), jnp.bfloat16),
            pltpu.VMEM(obs_list.shape[::-1], jnp.int32),
            pltpu.VMEM((ns, depth, width), jnp.bfloat16),
            plane, plane, params, params,
            pltpu.VMEM((ny, halves, hours, LANES), f32),
            pltpu.VMEM((ny, halves, hours, LANES), f32),
            pltpu.VMEM((ny, halves, hours, LANES), f32),
            pltpu.VMEM((max(ny - 1, 1), halves, hours, LANES), f32),
            tiles, tiles, tiles, tiles, tiles, tiles, tiles, tiles,
            pltpu.VMEM((nt, halves, 4, LANES), f32),
            pltpu.VMEM((halves, nt, 2, LANES), f32),
            plane, plane,
            dma((CHUNKS,)), dma((CHUNKS,)), dma((ns,)), dma, dma((halves,)), dma((halves,)), dma((2,)),
            dma((ny, halves)), dma((ny, halves)), dma((ny, halves)), dma((ny, halves)),
            dma((nt,)), dma((nt,)), dma((halves, nt)), dma((halves, nt)),
        ],
        compiler_params=pltpu.CompilerParams(
            collective_id=0, has_side_effects=True, vmem_limit_bytes=56 * 1024 * 1024
        ),
        cost_estimate=pl.CostEstimate(
            flops=2 * hours * depth * modes, bytes_accessed=2 * depth * (hours + modes), transcendentals=0
        ),
    )(
        observations, obs_list.T, gain_rows, decay, smooth_gain,
        model_rate.reshape(modes // LANES, LANES), first_state.reshape(modes // LANES, LANES),
    )


def solution(mesh):
    nt, ns = mesh.shape["tm"], mesh.shape["sensor"]
    in_specs = (
        P("tm", "sensor"),
        P("tm", "sensor"),
        P("sensor", None),
        P("tm", None),
        P("tm", None),
        P(),
        P(),
    )
    out_specs = (P("tm", "sensor"), P("tm", "sensor"))
    return jax.shard_map(
        functools.partial(per_device, nt, ns),
        mesh=mesh, in_specs=in_specs, out_specs=out_specs, check_vma=False,
    )
```

```python
import functools
import jax
import jax.numpy as jnp
from jax import lax
from jax.experimental import pallas as pl
from jax.experimental.pallas import tpu as pltpu
from jax.sharding import PartitionSpec as P

LANES = 128
SEGS = 8
CHUNKS = 4
MESH = pl.DeviceIdType.MESH


def shift_rows(value, count, fill):
    rows = lax.broadcasted_iota(jnp.int32, value.shape, 0)
    moved = pltpu.roll(value, count % SEGS, 0)
    inside = (rows >= count) if count > 0 else (rows < SEGS + count)
    return jnp.where(inside, moved, jnp.float32(fill))


def factor_levels(factor, sign):
    levels = []
    for count in (1, 2, 4):
        levels.append(factor)
        factor = factor * shift_rows(factor, sign * count, 1.0)
    return levels, factor


def chain_rows(levels, value, sign):
    for level, count in zip(levels, (1, 2, 4)):
        value = value + level * shift_rows(value, sign * count, 0.0)
    return value


def kernel(
    nt, ny,
    obs, olist, gain, decay, sgain, rate, first,
    filt_out, smooth_out,
    obs_v, list_v, gain_v, dec_v, sg_v, rate_v, first_v,
    csend, crecv, acc, yrecv,
    um, fm, am, dm, gm, cm, pm, qm,
    early, late, part_send, part_recv, filt_v, smooth_v,
    obs_sem, gain0_sem, gain_sem, list_sem, dec_sem, sg_sem, par_sem,
    cs_sem, cr_sem, ys_sem, yr_sem, ps_sem, pr_sem, es_sem, er_sem, ls_sem, lr_sem,
):
    tm = lax.axis_index("tm")
    sensor = lax.axis_index("sensor")
    y = sensor // 2
    core = sensor % 2
    partner = sensor + 1 - 2 * core
    hours, depth = obs_v.shape
    halves = acc.shape[1]
    width = halves * LANES
    blocks = depth // LANES
    steps = hours // SEGS
    chunk = depth // CHUNKS
    shifts = list(range(1, ny)) + [0]
    last = ny - 1

    def mine_at(k):
        return lax.rem(y + k, ny) * 2 + core

    def columns(dest, j):
        return pl.ds(pl.multiple_of(dest * width + j * LANES, LANES), LANES)

    def gain_pair(n, j, rows, sems):
        own = mine_at(shifts[n])
        other = own + 1 - 2 * core
        slot = gain_v.at[n * halves + j]
        return [
            pltpu.make_async_copy(
                gain.at[rows, columns(dest, j)], slot.at[rows, pl.ds(side * LANES, LANES)], sems.at[side]
            )
            for side, dest in enumerate((other, own))
        ]

    list_copy = pltpu.make_async_copy(olist, list_v, list_sem)
    list_copy.start()
    obs_copies, gain0_copies = [], []
    for n in range(CHUNKS):
        part = pl.ds(n * chunk, chunk)
        obs_copies.append(pltpu.make_async_copy(obs.at[:, part], obs_v.at[:, part], obs_sem.at[n]))
        gain0_copies.append(gain_pair(0, 0, part, gain0_sem.at[n]))
        for copy in [obs_copies[-1]] + gain0_copies[-1]:
            copy.start()
    everything = pl.ds(0, depth)
    gain_copies = {
        (n, j): gain_pair(n, j, everything, gain_sem.at[n * halves + j])
        for n in range(ny) for j in range(halves) if n + j > 0
    }
    pairs = list(gain_copies)
    steady_copies = []
    for n in range(ny):
        for j in range(halves):
            here = columns(mine_at(shifts[n]), j)
            steady_copies.append(pltpu.make_async_copy(decay.at[:, here], dec_v.at[n, j], dec_sem.at[n, j]))
            steady_copies.append(pltpu.make_async_copy(sgain.at[:, here], sg_v.at[n, j], sg_sem.at[n, j]))
    steady_copies.append(pltpu.make_async_copy(rate, rate_v, par_sem.at[0]))
    steady_copies.append(pltpu.make_async_copy(first, first_v, par_sem.at[1]))

    barrier = pltpu.get_barrier_semaphore()
    peers = [(tm, partner)]
    peers += [(tm, mine_at(k)) for k in range(1, ny)]
    peers += [(lax.rem(tm + k, nt), sensor) for k in range(1, nt)]
    for peer in peers:
        pl.semaphore_signal(barrier, inc=1, device_id=peer, device_id_type=MESH)

    list_copy.wait()
    place = list_v[...] - sensor * blocks
    valid = (place >= 0) & (place < blocks)
    bit = jnp.where(valid, lax.shift_left(jnp.int32(1), jnp.where(valid, place, 0)), 0)
    flat = jnp.broadcast_to(jnp.sum(bit, axis=0, keepdims=True), (LANES, hours))
    bits = jnp.transpose(flat)

    def gate(b, carry):
        part = pl.ds(pl.multiple_of(b * LANES, LANES), LANES)
        listed = (bits & lax.shift_left(jnp.int32(1), b)) != 0
        value = obs_v[:, part].astype(jnp.float32)
        obs_v[:, part] = jnp.where(listed, value, 0.0).astype(jnp.bfloat16)
        return carry

    total = None
    for n in range(CHUNKS):
        obs_copies[n].wait()
        lax.fori_loop(n * (blocks // CHUNKS), (n + 1) * (blocks // CHUNKS), gate, 0)
        for copy in gain0_copies[n]:
            copy.wait()
        if n == CHUNKS // 2 - 1:
            for copy in gain_copies[pairs[0]]:
                copy.start()
        part = pl.ds(n * chunk, chunk)
        term = jnp.dot(obs_v[:, part], gain_v[0, part], preferred_element_type=jnp.float32)
        total = term if total is None else total + term
    for copy in steady_copies:
        copy.start()
    for pair in pairs[1:]:
        for copy in gain_copies[pair]:
            copy.start()

    core_copies, y_copies = {}, {}

    def hand_over(n, j, total):
        csend[n, j] = total[:, :LANES]
        copy = pltpu.make_async_remote_copy(
            csend.at[n, j], crecv.at[n, j], cs_sem.at[n, j], cr_sem.at[n, j],
            device_id=(tm, partner), device_id_type=MESH,
        )
        copy.start()
        core_copies[n, j] = copy
        acc[n, j] = total[:, LANES:]

    def product(n, j):
        for copy in gain_copies[n, j]:
            copy.wait()
        hand_over(
            n, j, jnp.dot(obs_v[...], gain_v[n * halves + j], preferred_element_type=jnp.float32)
        )

    def join(n, j):
        core_copies[n, j].wait_recv()
        acc[n, j] = acc[n, j] + crecv[n, j]

    def send_y(n, j):
        join(n, j)
        copy = pltpu.make_async_remote_copy(
            acc.at[n, j], yrecv.at[n, j], ys_sem.at[n, j], yr_sem.at[n, j],
            device_id=(tm, mine_at(shifts[n])), device_id_type=MESH,
        )
        copy.start()
        y_copies[n, j] = copy

    away = [(n, j) for n in range(last) for j in range(halves)]
    home = [(last, j) for j in range(halves)]
    pl.semaphore_wait(barrier, len(peers))
    hand_over(0, 0, total)
    if away:
        send_y(0, 0)
    for n, j in away[1:]:
        product(n, j)

    for copy in steady_copies:
        copy.wait()
    row_ids = lax.broadcasted_iota(jnp.int32, (SEGS, LANES), 0)
    last_row = (row_ids == SEGS - 1) & (tm == nt - 1)
    ones = jnp.ones((SEGS, LANES), jnp.float32)
    zeros = jnp.zeros((SEGS, LANES), jnp.float32)
    rates = {
        (n, j): jnp.broadcast_to(rate_v[pl.ds(mine_at(shifts[n]) * halves + j, 1), :], (SEGS, LANES))
        for n, j in away + home
    }
    prod = {at: ones for at in away + home}
    for i in range(steps):
        for at in away + home:
            d = dec_v[at[0], at[1], pl.ds(i, SEGS, stride=steps), :]
            prod[at] = d * prod[at]
            dm[at[0], at[1], i] = d
            pm[at[0], at[1], i] = prod[at]
    back = {at: ones for at in away + home}
    linear = {at: zeros for at in away + home}
    for i in reversed(range(steps)):
        for at in away + home:
            n, j = at
            g = sg_v[n, j, pl.ds(i, SEGS, stride=steps), :]
            if i == steps - 1:
                g = jnp.where(last_row, 0.0, g)
            c = 1.0 - g * rates[at]
            linear[at] = g * linear[at] + c * pm[n, j, i]
            back[at] = g * back[at]
            gm[n, j, i] = g
            cm[n, j, i] = c
            if n == last:
                qm[j, i] = back[at]
    p_levels, q_levels, p_before, q_after = {}, {}, {}, {}
    for at in away + home:
        p_levels[at], p_all = factor_levels(prod[at], 1)
        q_levels[at], q_all = factor_levels(back[at], -1)
        p_before[at] = shift_rows(p_all, 1, 1.0)
        q_after[at] = shift_rows(q_all, -1, 1.0)
        if at[0] == last:
            b_all = chain_rows(q_levels[at], linear[at] * p_before[at], -1)
            early[tm, at[1], 0:1] = p_all[SEGS - 1:SEGS]
            early[tm, at[1], 1:2] = q_all[0:1]
            early[tm, at[1], 2:3] = b_all[0:1]
            early[tm, at[1], 3:4] = jnp.zeros((1, LANES), jnp.float32)
    for at in away[1:]:
        send_y(*at)

    def summaries(group):
        state = {at: zeros for at in group}
        for i in range(steps):
            for at in group:
                n, j = at
                inflow = acc[n, j, pl.ds(i, SEGS, stride=steps), :]
                if n == last:
                    um[j, i] = inflow
                state[at] = dm[n, j, i] * state[at] + inflow
                fm[n, j, i] = state[at]
        back = {at: zeros for at in group}
        for i in reversed(range(steps)):
            for at in group:
                n, j = at
                back[at] = gm[n, j, i] * back[at] + cm[n, j, i] * fm[n, j, i]
        result = {}
        for at in group:
            f_all = chain_rows(p_levels[at], state[at], 1)
            f_before = shift_rows(f_all, 1, 0.0)
            a_all = chain_rows(q_levels[at], back[at] + linear[at] * f_before, -1)
            result[at] = (f_all[SEGS - 1:SEGS], a_all[0:1])
        return result

    part_copies = []
    away_result = summaries(away)
    for n in range(last):
        for j in range(halves):
            part_send[n, j, 0:1], part_send[n, j, 1:2] = away_result[n, j]
        copy = pltpu.make_async_remote_copy(
            part_send.at[n], part_recv.at[n], ps_sem.at[n], pr_sem.at[n],
            device_id=(tm, mine_at(shifts[n])), device_id_type=MESH,
        )
        copy.start()
        part_copies.append(copy)
    early_copies = []
    for k in range(1, nt):
        copy = pltpu.make_async_remote_copy(
            early.at[tm], early.at[tm], es_sem.at[k], er_sem.at[k],
            device_id=(lax.rem(tm + k, nt), sensor), device_id_type=MESH,
        )
        copy.start()
        early_copies.append(copy)

    for at in home:
        if at != (0, 0):
            product(*at)
    for at in home:
        join(*at)
    home_result = summaries(home)
    for copy in part_copies:
        copy.wait_recv()
    for n, j in home:
        f_row, a_row = home_result[n, j]
        for source in range(last):
            f_row = f_row + part_recv[source, j, 0:1]
            a_row = a_row + part_recv[source, j, 1:2]
        late[tm, j, 0:1] = f_row
        late[tm, j, 1:2] = a_row
    late_copies = []
    for k in range(1, nt):
        copy = pltpu.make_async_remote_copy(
            late.at[tm], late.at[tm], ls_sem.at[k], lr_sem.at[k],
            device_id=(lax.rem(tm + k, nt), sensor), device_id_type=MESH,
        )
        copy.start()
        late_copies.append(copy)
    for copy in early_copies + late_copies:
        copy.wait_recv()

    bounds = []
    for j in range(halves):
        entry = first_v[pl.ds(sensor * halves + j, 1), :]
        entries, mine = [], entry
        for t in range(nt):
            mine = jnp.where(tm == t, entry, mine)
            entries.append(entry)
            entry = early[t, j, 0:1] * entry + late[t, j, 0:1]
        after = jnp.zeros((1, LANES), jnp.float32)
        mine_after = after
        for t in reversed(range(nt)):
            mine_after = jnp.where(tm == t, after, mine_after)
            after = early[t, j, 1:2] * after + (late[t, j, 1:2] + early[t, j, 2:3] * entries[t])
        bounds.append((mine, mine_after))

    for j in range(halves):
        at = (last, j)
        mine, mine_after = bounds[j]
        for n in range(last):
            y_copies[n, j].wait_recv()
        state = zeros
        for i in range(steps):
            inflow = um[j, i]
            for n in range(last):
                inflow = inflow + yrecv[n, j, pl.ds(i, SEGS, stride=steps), :]
            state = dm[last, j, i] * state + inflow
            fm[last, j, i] = state
        f_before = shift_rows(chain_rows(p_levels[at], state, 1), 1, 0.0)
        seg_entry = p_before[at] * mine + f_before
        back = zeros
        for i in reversed(range(steps)):
            filtered = fm[last, j, i] + pm[last, j, i] * seg_entry
            filt_v[j, pl.ds(i, SEGS, stride=steps), :] = filtered
            back = gm[last, j, i] * back + cm[last, j, i] * filtered
            am[j, i] = back
        a_after = shift_rows(chain_rows(q_levels[at], back, -1), -1, 0.0)
        seg_after = q_after[at] * mine_after + a_after
        for i in range(steps):
            smooth_v[j, pl.ds(i, SEGS, stride=steps), :] = am[j, i] + qm[j, i] * seg_after
        filt_out[:, j * LANES:(j + 1) * LANES] = filt_v[j]
        smooth_out[:, j * LANES:(j + 1) * LANES] = smooth_v[j]

    for copy in list(core_copies.values()) + list(y_copies.values()):
        copy.wait_send()
    for copy in part_copies + early_copies + late_copies:
        copy.wait_send()


def per_device(nt, ns, observations, obs_list, gain_rows, decay, smooth_gain, model_rate, first_state):
    ny = ns // 2
    hours, depth = observations.shape
    modes = gain_rows.shape[1]
    width = modes // ns
    halves = width // LANES
    steps = hours // SEGS
    f32 = jnp.float32
    dma = pltpu.SemaphoreType.DMA
    any_space = pl.BlockSpec(memory_space=pl.ANY)
    tiles = pltpu.VMEM((halves, steps, SEGS, LANES), f32)
    plane = pltpu.VMEM((halves, hours, LANES), f32)
    planes = pltpu.VMEM((ny, halves, hours, LANES), f32)
    group_tiles = pltpu.VMEM((ny, halves, steps, SEGS, LANES), f32)
    params = pltpu.VMEM((modes // LANES, LANES), f32)
    out = pltpu.VMEM((hours, width), f32)
    vmem_space = pl.BlockSpec(memory_space=pltpu.VMEM)
    return pl.pallas_call(
        functools.partial(kernel, nt, ny),
        out_shape=(out, out),
        in_specs=[any_space] * 7,
        out_specs=(vmem_space, vmem_space),
        scratch_shapes=[
            pltpu.VMEM((hours, depth), jnp.bfloat16),
            pltpu.VMEM(obs_list.shape[::-1], jnp.int32),
            pltpu.VMEM((ny * halves, depth, 2 * LANES), jnp.bfloat16),
            planes, planes, params, params,
            planes, planes, planes, planes,
            tiles, group_tiles, tiles, group_tiles, group_tiles, group_tiles, group_tiles, tiles,
            pltpu.VMEM((nt, halves, 4, LANES), f32),
            pltpu.VMEM((nt, halves, 2, LANES), f32),
            pltpu.VMEM((ny, halves, 2, LANES), f32),
            pltpu.VMEM((ny, halves, 2, LANES), f32),
            plane, plane,
            dma((CHUNKS,)), dma((CHUNKS, 2)), dma((ny * halves, 2)), dma, dma((ny, halves)), dma((ny, halves)), dma((2,)),
            dma((ny, halves)), dma((ny, halves)), dma((ny, halves)), dma((ny, halves)),
            dma((ny,)), dma((ny,)), dma((nt,)), dma((nt,)), dma((nt,)), dma((nt,)),
        ],
        compiler_params=pltpu.CompilerParams(
            collective_id=0, has_side_effects=True, vmem_limit_bytes=56 * 1024 * 1024
        ),
        cost_estimate=pl.CostEstimate(
            flops=2 * hours * depth * modes, bytes_accessed=2 * depth * (hours + modes), transcendentals=0
        ),
    )(
        observations, obs_list.T, gain_rows, decay, smooth_gain,
        model_rate.reshape(modes // LANES, LANES), first_state.reshape(modes // LANES, LANES),
    )


def solution(mesh):
    nt, ns = mesh.shape["tm"], mesh.shape["sensor"]
    in_specs = (
        P("tm", "sensor"),
        P("tm", "sensor"),
        P("sensor", None),
        P("tm", None),
        P("tm", None),
        P(),
        P(),
    )
    out_specs = (P("tm", "sensor"), P("tm", "sensor"))
    return jax.shard_map(
        functools.partial(per_device, nt, ns),
        mesh=mesh, in_specs=in_specs, out_specs=out_specs, check_vma=False,
    )
```

```python
import functools
import jax
import jax.numpy as jnp
from jax import lax
from jax.experimental import pallas as pl
from jax.experimental.pallas import tpu as pltpu
from jax.sharding import PartitionSpec as P

LANES = 128
SEGS = 8
CHUNKS = 4
MESH = pl.DeviceIdType.MESH


def shift_rows(value, count, fill):
    rows = lax.broadcasted_iota(jnp.int32, value.shape, 0)
    moved = pltpu.roll(value, count % SEGS, 0)
    inside = (rows >= count) if count > 0 else (rows < SEGS + count)
    return jnp.where(inside, moved, jnp.float32(fill))


def factor_levels(factor, sign):
    levels = []
    for count in (1, 2, 4):
        levels.append(factor)
        factor = factor * shift_rows(factor, sign * count, 1.0)
    return levels, factor


def chain_rows(levels, value, sign):
    for level, count in zip(levels, (1, 2, 4)):
        value = value + level * shift_rows(value, sign * count, 0.0)
    return value


def kernel(
    nt, ny,
    obs, olist, gain, decay, sgain, rate, first,
    filt_out, smooth_out,
    obs_v, list_v, gain_v, dec_v, sg_v, rate_v, first_v,
    csend, crecv, acc, yrecv,
    um, fm, am, dm, gm, cm, pm, qm, bm,
    early, late, part_send, part_recv, filt_v, smooth_v,
    obs_sem, gain0_sem, gain_sem, list_sem, dec_sem, sg_sem, par_sem,
    cs_sem, cr_sem, ys_sem, yr_sem, ps_sem, pr_sem, es_sem, er_sem, ls_sem, lr_sem,
):
    tm = lax.axis_index("tm")
    sensor = lax.axis_index("sensor")
    y = sensor // 2
    core = sensor % 2
    partner = sensor + 1 - 2 * core
    hours, depth = obs_v.shape
    halves = acc.shape[1]
    width = halves * LANES
    blocks = depth // LANES
    steps = hours // SEGS
    chunk = depth // CHUNKS
    shifts = list(range(1, ny)) + [0]
    last = ny - 1

    def mine_at(k):
        return lax.rem(y + k, ny) * 2 + core

    def columns(dest, j):
        return pl.ds(pl.multiple_of(dest * width + j * LANES, LANES), LANES)

    def gain_pair(n, j, rows, sems):
        own = mine_at(shifts[n])
        other = own + 1 - 2 * core
        slot = gain_v.at[n * halves + j]
        return [
            pltpu.make_async_copy(
                gain.at[rows, columns(dest, j)], slot.at[rows, pl.ds(side * LANES, LANES)], sems.at[side]
            )
            for side, dest in enumerate((other, own))
        ]

    list_copy = pltpu.make_async_copy(olist, list_v, list_sem)
    list_copy.start()
    obs_copies, gain0_copies = [], []
    for n in range(CHUNKS):
        part = pl.ds(n * chunk, chunk)
        obs_copies.append(pltpu.make_async_copy(obs.at[:, part], obs_v.at[:, part], obs_sem.at[n]))
        gain0_copies.append(gain_pair(0, 0, part, gain0_sem.at[n]))
        for copy in [obs_copies[-1]] + gain0_copies[-1]:
            copy.start()
    everything = pl.ds(0, depth)
    gain_copies = {
        (n, j): gain_pair(n, j, everything, gain_sem.at[n * halves + j])
        for n in range(ny) for j in range(halves) if n + j > 0
    }
    pairs = list(gain_copies)
    steady_copies = []
    for n in range(ny):
        for j in range(halves):
            here = columns(mine_at(shifts[n]), j)
            steady_copies.append(pltpu.make_async_copy(decay.at[:, here], dec_v.at[n, j], dec_sem.at[n, j]))
            steady_copies.append(pltpu.make_async_copy(sgain.at[:, here], sg_v.at[n, j], sg_sem.at[n, j]))
    steady_copies.append(pltpu.make_async_copy(rate, rate_v, par_sem.at[0]))
    steady_copies.append(pltpu.make_async_copy(first, first_v, par_sem.at[1]))

    barrier = pltpu.get_barrier_semaphore()
    peers = [(tm, partner)]
    peers += [(tm, mine_at(k)) for k in range(1, ny)]
    peers += [(lax.rem(tm + k, nt), sensor) for k in range(1, nt)]
    for peer in peers:
        pl.semaphore_signal(barrier, inc=1, device_id=peer, device_id_type=MESH)

    list_copy.wait()
    place = list_v[...] - sensor * blocks
    valid = (place >= 0) & (place < blocks)
    bit = jnp.where(valid, lax.shift_left(jnp.int32(1), jnp.where(valid, place, 0)), 0)
    flat = jnp.broadcast_to(jnp.sum(bit, axis=0, keepdims=True), (LANES, hours))
    bits = jnp.transpose(flat)

    low_bits = (bits & 0xFFFF).astype(jnp.int16)
    high_bits = lax.shift_right_logical(bits, 16).astype(jnp.int16)

    def gated(b):
        part = obs_v[:, b * LANES:(b + 1) * LANES]
        word, place = (low_bits, b) if b < 16 else (high_bits, b - 16)
        flag = jnp.int16((1 << place) if place < 15 else -32768)
        return jnp.where((word & flag) != 0, part, jnp.bfloat16(0))

    total = None
    for n in range(CHUNKS):
        obs_copies[n].wait()
        for copy in gain0_copies[n]:
            copy.wait()
        if n == CHUNKS // 2 - 1:
            for copy in gain_copies[pairs[0]]:
                copy.start()
        part = pl.ds(n * chunk, chunk)
        per = blocks // CHUNKS
        weighted = jnp.concatenate([gated(b) for b in range(n * per, (n + 1) * per)], axis=1)
        obs_v[:, part] = weighted
        term = jnp.dot(weighted, gain_v[0, part], preferred_element_type=jnp.float32)
        total = term if total is None else total + term
    for copy in steady_copies:
        copy.start()
    for pair in pairs[1:]:
        for copy in gain_copies[pair]:
            copy.start()

    core_copies, y_copies = {}, {}

    def hand_over(n, j, total):
        csend[n, j] = total[:, :LANES]
        copy = pltpu.make_async_remote_copy(
            csend.at[n, j], crecv.at[n, j], cs_sem.at[n, j], cr_sem.at[n, j],
            device_id=(tm, partner), device_id_type=MESH,
        )
        copy.start()
        core_copies[n, j] = copy
        acc[n, j] = total[:, LANES:]

    def product(n, j):
        return jnp.dot(obs_v[...], gain_v[n * halves + j], preferred_element_type=jnp.float32)

    def wait_gain(*pairs):
        for pair in pairs:
            for copy in gain_copies[pair]:
                copy.wait()

    def join(n, j):
        core_copies[n, j].wait_recv()
        acc[n, j] = acc[n, j] + crecv[n, j]

    def send_y(n, j):
        join(n, j)
        copy = pltpu.make_async_remote_copy(
            acc.at[n, j], yrecv.at[n, j], ys_sem.at[n, j], yr_sem.at[n, j],
            device_id=(tm, mine_at(shifts[n])), device_id_type=MESH,
        )
        copy.start()
        y_copies[n, j] = copy

    away = [(n, j) for n in range(last) for j in range(halves)]
    home = [(last, j) for j in range(halves)]
    pl.semaphore_wait(barrier, len(peers))
    hand_over(0, 0, total)
    if away:
        send_y(0, 0)

    wait_gain(*away[1:])
    for copy in steady_copies:
        copy.wait()
    row_ids = lax.broadcasted_iota(jnp.int32, (SEGS, LANES), 0)
    products = {at: product(*at) for at in away[1:]}
    last_row = (row_ids == SEGS - 1) & (tm == nt - 1)
    ones = jnp.ones((SEGS, LANES), jnp.float32)
    zeros = jnp.zeros((SEGS, LANES), jnp.float32)
    rates = {
        (n, j): jnp.broadcast_to(rate_v[pl.ds(mine_at(shifts[n]) * halves + j, 1), :], (SEGS, LANES))
        for n, j in away + home
    }
    prod = {at: ones for at in away + home}
    for i in range(steps):
        for at in away + home:
            d = dec_v[at[0], at[1], pl.ds(i, SEGS, stride=steps), :]
            prod[at] = d * prod[at]
            dm[at[0], at[1], i] = d
            pm[at[0], at[1], i] = prod[at]
    back = {at: ones for at in away + home}
    linear = {at: zeros for at in away + home}
    for i in reversed(range(steps)):
        for at in away + home:
            n, j = at
            g = sg_v[n, j, pl.ds(i, SEGS, stride=steps), :]
            if i == steps - 1:
                g = jnp.where(last_row, 0.0, g)
            c = 1.0 - g * rates[at]
            linear[at] = g * linear[at] + c * pm[n, j, i]
            back[at] = g * back[at]
            gm[n, j, i] = g
            cm[n, j, i] = c
            if n == last:
                qm[j, i] = back[at]
                bm[j, i] = linear[at]
    p_levels, q_levels, p_before, q_after, b_after = {}, {}, {}, {}, {}
    for at in away + home:
        p_levels[at], p_all = factor_levels(prod[at], 1)
        q_levels[at], q_all = factor_levels(back[at], -1)
        p_before[at] = shift_rows(p_all, 1, 1.0)
        q_after[at] = shift_rows(q_all, -1, 1.0)
        if at[0] == last:
            b_all = chain_rows(q_levels[at], linear[at] * p_before[at], -1)
            b_after[at] = shift_rows(b_all, -1, 0.0)
            early[tm, at[1], 0:1] = p_all[SEGS - 1:SEGS]
            early[tm, at[1], 1:2] = q_all[0:1]
            early[tm, at[1], 2:3] = b_all[0:1]
            early[tm, at[1], 3:4] = jnp.zeros((1, LANES), jnp.float32)
    for at in away[1:]:
        hand_over(*at, products[at])
    ahead = [at for at in home[:1] if at != (0, 0)]
    wait_gain(*ahead)
    for at in ahead:
        hand_over(*at, product(*at))
    for at in away[1:]:
        send_y(*at)
    behind = home[1:]
    wait_gain(*behind)
    products = {at: product(*at) for at in behind}

    def summaries(group):
        state = {at: zeros for at in group}
        for i in range(steps):
            for at in group:
                n, j = at
                inflow = acc[n, j, pl.ds(i, SEGS, stride=steps), :]
                if n == last:
                    um[j, i] = inflow
                state[at] = dm[n, j, i] * state[at] + inflow
                fm[n, j, i] = state[at]
        back = {at: zeros for at in group}
        for i in reversed(range(steps)):
            for at in group:
                n, j = at
                back[at] = gm[n, j, i] * back[at] + cm[n, j, i] * fm[n, j, i]
        result = {}
        for at in group:
            f_all = chain_rows(p_levels[at], state[at], 1)
            f_before = shift_rows(f_all, 1, 0.0)
            a_all = chain_rows(q_levels[at], back[at] + linear[at] * f_before, -1)
            result[at] = (f_all[SEGS - 1:SEGS], a_all[0:1])
        return result

    part_copies = []
    away_result = summaries(away)
    for at in behind:
        hand_over(*at, products[at])
    for n in range(last):
        for j in range(halves):
            part_send[n, j, 0:1], part_send[n, j, 1:2] = away_result[n, j]
        copy = pltpu.make_async_remote_copy(
            part_send.at[n], part_recv.at[n], ps_sem.at[n], pr_sem.at[n],
            device_id=(tm, mine_at(shifts[n])), device_id_type=MESH,
        )
        copy.start()
        part_copies.append(copy)
    early_copies = []
    for k in range(1, nt):
        copy = pltpu.make_async_remote_copy(
            early.at[tm], early.at[tm], es_sem.at[k], er_sem.at[k],
            device_id=(lax.rem(tm + k, nt), sensor), device_id_type=MESH,
        )
        copy.start()
        early_copies.append(copy)

    for at in home:
        join(*at)
    home_result = summaries(home)
    for copy in part_copies:
        copy.wait_recv()
    for n, j in home:
        f_row, a_row = home_result[n, j]
        for source in range(last):
            f_row = f_row + part_recv[source, j, 0:1]
            a_row = a_row + part_recv[source, j, 1:2]
        late[tm, j, 0:1] = f_row
        late[tm, j, 1:2] = a_row
    late_copies = []
    for k in range(1, nt):
        copy = pltpu.make_async_remote_copy(
            late.at[tm], late.at[tm], ls_sem.at[k], lr_sem.at[k],
            device_id=(lax.rem(tm + k, nt), sensor), device_id_type=MESH,
        )
        copy.start()
        late_copies.append(copy)
    f_before, a_after = {}, {}
    for at in home:
        j = at[1]
        for n in range(last):
            y_copies[n, j].wait_recv()
        state = zeros
        for i in range(steps):
            inflow = um[j, i]
            for n in range(last):
                inflow = inflow + yrecv[n, j, pl.ds(i, SEGS, stride=steps), :]
            state = dm[last, j, i] * state + inflow
            fm[last, j, i] = state
        back = zeros
        for i in reversed(range(steps)):
            back = gm[last, j, i] * back + cm[last, j, i] * fm[last, j, i]
            am[j, i] = back
        f_before[at] = shift_rows(chain_rows(p_levels[at], state, 1), 1, 0.0)
        a_all = chain_rows(q_levels[at], back + linear[at] * f_before[at], -1)
        a_after[at] = shift_rows(a_all, -1, 0.0)

    for copy in early_copies + late_copies:
        copy.wait_recv()
    for at in home:
        j = at[1]
        entry = first_v[pl.ds(sensor * halves + j, 1), :]
        entries, mine = [], entry
        for t in range(nt):
            mine = jnp.where(tm == t, entry, mine)
            entries.append(entry)
            entry = early[t, j, 0:1] * entry + late[t, j, 0:1]
        after = jnp.zeros((1, LANES), jnp.float32)
        mine_after = after
        for t in reversed(range(nt)):
            mine_after = jnp.where(tm == t, after, mine_after)
            after = early[t, j, 1:2] * after + (late[t, j, 1:2] + early[t, j, 2:3] * entries[t])
        seg_entry = p_before[at] * mine + f_before[at]
        seg_after = q_after[at] * mine_after + (a_after[at] + b_after[at] * mine)
        for i in range(steps):
            rows = pl.ds(i, SEGS, stride=steps)
            filt_v[j, rows, :] = fm[last, j, i] + pm[last, j, i] * seg_entry
            smooth_v[j, rows, :] = am[j, i] + bm[j, i] * seg_entry + qm[j, i] * seg_after
        filt_out[:, j * LANES:(j + 1) * LANES] = filt_v[j]
        smooth_out[:, j * LANES:(j + 1) * LANES] = smooth_v[j]

    for copy in list(core_copies.values()) + list(y_copies.values()):
        copy.wait_send()
    for copy in part_copies + early_copies + late_copies:
        copy.wait_send()


def per_device(nt, ns, observations, obs_list, gain_rows, decay, smooth_gain, model_rate, first_state):
    ny = ns // 2
    hours, depth = observations.shape
    modes = gain_rows.shape[1]
    width = modes // ns
    halves = width // LANES
    steps = hours // SEGS
    f32 = jnp.float32
    dma = pltpu.SemaphoreType.DMA
    any_space = pl.BlockSpec(memory_space=pl.ANY)
    tiles = pltpu.VMEM((halves, steps, SEGS, LANES), f32)
    plane = pltpu.VMEM((halves, hours, LANES), f32)
    planes = pltpu.VMEM((ny, halves, hours, LANES), f32)
    group_tiles = pltpu.VMEM((ny, halves, steps, SEGS, LANES), f32)
    params = pltpu.VMEM((modes // LANES, LANES), f32)
    out = pltpu.VMEM((hours, width), f32)
    vmem_space = pl.BlockSpec(memory_space=pltpu.VMEM)
    return pl.pallas_call(
        functools.partial(kernel, nt, ny),
        out_shape=(out, out),
        in_specs=[any_space] * 7,
        out_specs=(vmem_space, vmem_space),
        scratch_shapes=[
            pltpu.VMEM((hours, depth), jnp.bfloat16),
            pltpu.VMEM(obs_list.shape[::-1], jnp.int32),
            pltpu.VMEM((ny * halves, depth, 2 * LANES), jnp.bfloat16),
            planes, planes, params, params,
            planes, planes, planes, planes,
            tiles, group_tiles, tiles, group_tiles, group_tiles, group_tiles, group_tiles, tiles, tiles,
            pltpu.VMEM((nt, halves, 4, LANES), f32),
            pltpu.VMEM((nt, halves, 2, LANES), f32),
            pltpu.VMEM((ny, halves, 2, LANES), f32),
            pltpu.VMEM((ny, halves, 2, LANES), f32),
            plane, plane,
            dma((CHUNKS,)), dma((CHUNKS, 2)), dma((ny * halves, 2)), dma, dma((ny, halves)), dma((ny, halves)), dma((2,)),
            dma((ny, halves)), dma((ny, halves)), dma((ny, halves)), dma((ny, halves)),
            dma((ny,)), dma((ny,)), dma((nt,)), dma((nt,)), dma((nt,)), dma((nt,)),
        ],
        compiler_params=pltpu.CompilerParams(
            collective_id=0, has_side_effects=True, vmem_limit_bytes=56 * 1024 * 1024
        ),
        cost_estimate=pl.CostEstimate(
            flops=2 * hours * depth * modes, bytes_accessed=2 * depth * (hours + modes), transcendentals=0
        ),
    )(
        observations, obs_list.T, gain_rows, decay, smooth_gain,
        model_rate.reshape(modes // LANES, LANES), first_state.reshape(modes // LANES, LANES),
    )


def solution(mesh):
    nt, ns = mesh.shape["tm"], mesh.shape["sensor"]
    in_specs = (
        P("tm", "sensor"),
        P("tm", "sensor"),
        P("sensor", None),
        P("tm", None),
        P("tm", None),
        P(),
        P(),
    )
    out_specs = (P("tm", "sensor"), P("tm", "sensor"))
    return jax.shard_map(
        functools.partial(per_device, nt, ns),
        mesh=mesh, in_specs=in_specs, out_specs=out_specs, check_vma=False,
    )
```

```python
import functools
import jax
import jax.numpy as jnp
from jax import lax
from jax.experimental import pallas as pl
from jax.experimental.pallas import tpu as pltpu
from jax.sharding import PartitionSpec as P

LANES = 128
SEGS = 8
CHUNKS = 4
UNROLL = 4
MESH = pl.DeviceIdType.MESH


def shift_rows(value, count, fill):
    rows = lax.broadcasted_iota(jnp.int32, value.shape, 0)
    moved = pltpu.roll(value, count % SEGS, 0)
    inside = (rows >= count) if count > 0 else (rows < SEGS + count)
    return jnp.where(inside, moved, jnp.float32(fill))


def factor_levels(factor, sign):
    levels = []
    for count in (1, 2, 4):
        levels.append(factor)
        factor = factor * shift_rows(factor, sign * count, 1.0)
    return levels, factor


def chain_rows(levels, value, sign):
    for level, count in zip(levels, (1, 2, 4)):
        value = value + level * shift_rows(value, sign * count, 0.0)
    return value


def hours_loop(steps, body, carry, reverse=False):
    def group(n, carry):
        for u in range(UNROLL):
            i = n * UNROLL + u
            carry = body(steps - 1 - i if reverse else i, carry)
        return carry

    return lax.fori_loop(0, steps // UNROLL, group, carry)


def kernel(
    nt, ny,
    obs, olist, gain, decay, sgain, rate, first,
    filt_out, smooth_out,
    obs_v, list_v, gain_v, dec_v, sg_v, rate_v, first_v,
    csend, crecv, acc, yrecv,
    um, fm, am, dm, gm, cm, pm, qm, bm,
    early, late, part_send, part_recv, filt_v, smooth_v, total_v,
    obs_sem, gain0_sem, gain_sem, list_sem, dec_sem, sg_sem, par_sem,
    cs_sem, cr_sem, ys_sem, yr_sem, ps_sem, pr_sem, es_sem, er_sem, ls_sem, lr_sem,
):
    tm = lax.axis_index("tm")
    sensor = lax.axis_index("sensor")
    y = sensor // 2
    core = sensor % 2
    partner = sensor + 1 - 2 * core
    hours, depth = obs_v.shape
    halves = acc.shape[1]
    width = halves * LANES
    blocks = depth // LANES
    steps = hours // SEGS
    chunk = depth // CHUNKS
    shifts = list(range(1, ny)) + [0]
    last = ny - 1

    def mine_at(k):
        return lax.rem(y + k, ny) * 2 + core

    def columns(dest, j):
        return pl.ds(pl.multiple_of(dest * width + j * LANES, LANES), LANES)

    def gain_pair(n, j, rows, sems):
        own = mine_at(shifts[n])
        other = own + 1 - 2 * core
        slot = gain_v.at[n * halves + j]
        return [
            pltpu.make_async_copy(
                gain.at[rows, columns(dest, j)], slot.at[rows, pl.ds(side * LANES, LANES)], sems.at[side]
            )
            for side, dest in enumerate((other, own))
        ]

    list_copy = pltpu.make_async_copy(olist, list_v, list_sem)
    list_copy.start()
    obs_copies, gain0_copies = [], []
    for n in range(CHUNKS):
        part = pl.ds(n * chunk, chunk)
        obs_copies.append(pltpu.make_async_copy(obs.at[:, part], obs_v.at[:, part], obs_sem.at[n]))
        gain0_copies.append(gain_pair(0, 0, part, gain0_sem.at[n]))
        for copy in [obs_copies[-1]] + gain0_copies[-1]:
            copy.start()
    everything = pl.ds(0, depth)
    gain_copies = {
        (n, j): gain_pair(n, j, everything, gain_sem.at[n * halves + j])
        for n in range(ny) for j in range(halves) if n + j > 0
    }
    pairs = list(gain_copies)
    steady_copies = []
    for n in range(ny):
        for j in range(halves):
            here = columns(mine_at(shifts[n]), j)
            steady_copies.append(pltpu.make_async_copy(decay.at[:, here], dec_v.at[n, j], dec_sem.at[n, j]))
            steady_copies.append(pltpu.make_async_copy(sgain.at[:, here], sg_v.at[n, j], sg_sem.at[n, j]))
    steady_copies.append(pltpu.make_async_copy(rate, rate_v, par_sem.at[0]))
    steady_copies.append(pltpu.make_async_copy(first, first_v, par_sem.at[1]))

    barrier = pltpu.get_barrier_semaphore()
    peers = [(tm, partner)]
    peers += [(tm, mine_at(k)) for k in range(1, ny)]
    peers += [(lax.rem(tm + k, nt), sensor) for k in range(1, nt)]
    for peer in peers:
        pl.semaphore_signal(barrier, inc=1, device_id=peer, device_id_type=MESH)

    list_copy.wait()
    place = list_v[...] - sensor * blocks
    valid = (place >= 0) & (place < blocks)
    bit = jnp.where(valid, lax.shift_left(jnp.int32(1), jnp.where(valid, place, 0)), 0)
    flat = jnp.broadcast_to(jnp.sum(bit, axis=0, keepdims=True), (LANES, hours))
    bits = jnp.transpose(flat)

    per = blocks // CHUNKS

    def first_chunk(n, carry):
        start = pl.multiple_of(n * chunk, chunk)
        part = pl.ds(start, chunk)
        pltpu.make_async_copy(obs.at[:, part], obs_v.at[:, part], obs_sem.at[n]).wait()
        word = lax.shift_right_logical(bits, n * per).astype(jnp.int16)
        pieces = []
        for b in range(per):
            piece = obs_v[:, pl.ds(pl.multiple_of(start + b * LANES, LANES), LANES)]
            pieces.append(jnp.where((word & jnp.int16(1 << b)) != 0, piece, jnp.bfloat16(0)))
        weighted = jnp.concatenate(pieces, axis=1)
        obs_v[:, part] = weighted
        for copy in gain_pair(0, 0, part, gain0_sem.at[n]):
            copy.wait()
        term = jnp.dot(weighted, gain_v[0, part], preferred_element_type=jnp.float32)

        @pl.when(n == 0)
        def _():
            total_v[...] = term

        @pl.when(n > 0)
        def _():
            total_v[...] += term

        @pl.when(n == CHUNKS // 2 - 1)
        def _():
            for copy in gain_copies[pairs[0]]:
                copy.start()

        return carry

    lax.fori_loop(0, CHUNKS, first_chunk, 0)
    for copy in steady_copies:
        copy.start()
    for pair in pairs[1:]:
        for copy in gain_copies[pair]:
            copy.start()

    core_copies, y_copies = {}, {}

    def hand_over(n, j):
        csend[n, j] = total_v[:, :LANES]
        copy = pltpu.make_async_remote_copy(
            csend.at[n, j], crecv.at[n, j], cs_sem.at[n, j], cr_sem.at[n, j],
            device_id=(tm, partner), device_id_type=MESH,
        )
        copy.start()
        core_copies[n, j] = copy
        acc[n, j] = total_v[:, LANES:]

    def product(n, j):
        total_v[...] = jnp.zeros_like(total_v)

        def add(m, carry):
            part = pl.ds(pl.multiple_of(m * chunk, chunk), chunk)
            total_v[...] += jnp.dot(
                obs_v[:, part], gain_v[n * halves + j, part], preferred_element_type=jnp.float32
            )
            return carry

        lax.fori_loop(0, CHUNKS, add, 0)
        hand_over(n, j)

    def wait_gain(*pairs):
        for pair in pairs:
            for copy in gain_copies[pair]:
                copy.wait()

    def join(n, j):
        core_copies[n, j].wait_recv()
        acc[n, j] = acc[n, j] + crecv[n, j]

    def send_y(n, j):
        join(n, j)
        copy = pltpu.make_async_remote_copy(
            acc.at[n, j], yrecv.at[n, j], ys_sem.at[n, j], yr_sem.at[n, j],
            device_id=(tm, mine_at(shifts[n])), device_id_type=MESH,
        )
        copy.start()
        y_copies[n, j] = copy

    away = [(n, j) for n in range(last) for j in range(halves)]
    home = [(last, j) for j in range(halves)]
    pl.semaphore_wait(barrier, len(peers))
    hand_over(0, 0)
    if away:
        send_y(0, 0)

    wait_gain(*away[1:])
    for at in away[1:]:
        product(*at)
    for copy in steady_copies:
        copy.wait()
    row_ids = lax.broadcasted_iota(jnp.int32, (SEGS, LANES), 0)
    last_row = (row_ids == SEGS - 1) & (tm == nt - 1)
    ones = jnp.ones((SEGS, LANES), jnp.float32)
    zeros = jnp.zeros((SEGS, LANES), jnp.float32)
    rates = {
        (n, j): jnp.broadcast_to(rate_v[pl.ds(mine_at(shifts[n]) * halves + j, 1), :], (SEGS, LANES))
        for n, j in away + home
    }
    spots = away + home

    def forward_factors(i, prods):
        out = []
        for (n, j), prod in zip(spots, prods):
            d = dec_v[n, j, pl.ds(i, SEGS, stride=steps), :]
            prod = d * prod
            dm[n, j, i] = d
            pm[n, j, i] = prod
            out.append(prod)
        return tuple(out)

    prods = hours_loop(steps, forward_factors, (ones,) * len(spots))

    def backward_factors(i, pairs):
        out = []
        for at, (line, factor) in zip(spots, pairs):
            n, j = at
            g = sg_v[n, j, pl.ds(i, SEGS, stride=steps), :]
            g = jnp.where(last_row & (i == steps - 1), 0.0, g)
            c = 1.0 - g * rates[at]
            line = g * line + c * pm[n, j, i]
            factor = g * factor
            gm[n, j, i] = g
            cm[n, j, i] = c
            if n == last:
                qm[j, i] = factor
                bm[j, i] = line
            out.append((line, factor))
        return tuple(out)

    factors = hours_loop(steps, backward_factors, ((zeros, ones),) * len(spots), reverse=True)
    prod = dict(zip(spots, prods))
    linear = {at: line for at, (line, _) in zip(spots, factors)}
    back = {at: factor for at, (_, factor) in zip(spots, factors)}
    p_levels, q_levels, p_before, q_after, b_after = {}, {}, {}, {}, {}
    for at in away + home:
        p_levels[at], p_all = factor_levels(prod[at], 1)
        q_levels[at], q_all = factor_levels(back[at], -1)
        p_before[at] = shift_rows(p_all, 1, 1.0)
        q_after[at] = shift_rows(q_all, -1, 1.0)
        if at[0] == last:
            b_all = chain_rows(q_levels[at], linear[at] * p_before[at], -1)
            b_after[at] = shift_rows(b_all, -1, 0.0)
            early[tm, at[1], 0:1] = p_all[SEGS - 1:SEGS]
            early[tm, at[1], 1:2] = q_all[0:1]
            early[tm, at[1], 2:3] = b_all[0:1]
            early[tm, at[1], 3:4] = jnp.zeros((1, LANES), jnp.float32)
    ahead = [at for at in home[:1] if at != (0, 0)]
    wait_gain(*ahead)
    for at in ahead:
        product(*at)
    for at in away[1:]:
        send_y(*at)
    behind = home[1:]
    wait_gain(*behind)
    for at in behind:
        product(*at)

    def summaries(group):
        def forward(i, states):
            out = []
            for (n, j), state in zip(group, states):
                inflow = acc[n, j, pl.ds(i, SEGS, stride=steps), :]
                if n == last:
                    um[j, i] = inflow
                state = dm[n, j, i] * state + inflow
                fm[n, j, i] = state
                out.append(state)
            return tuple(out)

        states = hours_loop(steps, forward, (zeros,) * len(group))

        def backward(i, backs):
            return tuple(
                gm[n, j, i] * back + cm[n, j, i] * fm[n, j, i] for (n, j), back in zip(group, backs)
            )

        backs = hours_loop(steps, backward, (zeros,) * len(group), reverse=True)
        state, back = dict(zip(group, states)), dict(zip(group, backs))
        result = {}
        for at in group:
            f_all = chain_rows(p_levels[at], state[at], 1)
            f_before = shift_rows(f_all, 1, 0.0)
            a_all = chain_rows(q_levels[at], back[at] + linear[at] * f_before, -1)
            result[at] = (f_all[SEGS - 1:SEGS], a_all[0:1])
        return result

    part_copies = []
    away_result = summaries(away)
    for n in range(last):
        for j in range(halves):
            part_send[n, j, 0:1], part_send[n, j, 1:2] = away_result[n, j]
        copy = pltpu.make_async_remote_copy(
            part_send.at[n], part_recv.at[n], ps_sem.at[n], pr_sem.at[n],
            device_id=(tm, mine_at(shifts[n])), device_id_type=MESH,
        )
        copy.start()
        part_copies.append(copy)
    early_copies = []
    for k in range(1, nt):
        copy = pltpu.make_async_remote_copy(
            early.at[tm], early.at[tm], es_sem.at[k], er_sem.at[k],
            device_id=(lax.rem(tm + k, nt), sensor), device_id_type=MESH,
        )
        copy.start()
        early_copies.append(copy)

    for at in home:
        join(*at)
    home_result = summaries(home)
    for copy in part_copies:
        copy.wait_recv()
    for n, j in home:
        f_row, a_row = home_result[n, j]
        for source in range(last):
            f_row = f_row + part_recv[source, j, 0:1]
            a_row = a_row + part_recv[source, j, 1:2]
        late[tm, j, 0:1] = f_row
        late[tm, j, 1:2] = a_row
    late_copies = []
    for k in range(1, nt):
        copy = pltpu.make_async_remote_copy(
            late.at[tm], late.at[tm], ls_sem.at[k], lr_sem.at[k],
            device_id=(lax.rem(tm + k, nt), sensor), device_id_type=MESH,
        )
        copy.start()
        late_copies.append(copy)
    f_before, a_after = {}, {}
    for at in home:
        j = at[1]
        for n in range(last):
            y_copies[n, j].wait_recv()

        def forward(i, state, j=j):
            inflow = um[j, i]
            for n in range(last):
                inflow = inflow + yrecv[n, j, pl.ds(i, SEGS, stride=steps), :]
            state = dm[last, j, i] * state + inflow
            fm[last, j, i] = state
            return state

        def backward(i, back, j=j):
            back = gm[last, j, i] * back + cm[last, j, i] * fm[last, j, i]
            am[j, i] = back
            return back

        state = hours_loop(steps, forward, zeros)
        back = hours_loop(steps, backward, zeros, reverse=True)
        f_before[at] = shift_rows(chain_rows(p_levels[at], state, 1), 1, 0.0)
        a_all = chain_rows(q_levels[at], back + linear[at] * f_before[at], -1)
        a_after[at] = shift_rows(a_all, -1, 0.0)

    for copy in early_copies + late_copies:
        copy.wait_recv()
    for at in home:
        j = at[1]
        entry = first_v[pl.ds(sensor * halves + j, 1), :]
        entries, mine = [], entry
        for t in range(nt):
            mine = jnp.where(tm == t, entry, mine)
            entries.append(entry)
            entry = early[t, j, 0:1] * entry + late[t, j, 0:1]
        after = jnp.zeros((1, LANES), jnp.float32)
        mine_after = after
        for t in reversed(range(nt)):
            mine_after = jnp.where(tm == t, after, mine_after)
            after = early[t, j, 1:2] * after + (late[t, j, 1:2] + early[t, j, 2:3] * entries[t])
        seg_entry = p_before[at] * mine + f_before[at]
        seg_after = q_after[at] * mine_after + (a_after[at] + b_after[at] * mine)

        def finish(i, carry, j=j, seg_entry=seg_entry, seg_after=seg_after):
            rows = pl.ds(i, SEGS, stride=steps)
            filt_v[j, rows, :] = fm[last, j, i] + pm[last, j, i] * seg_entry
            smooth_v[j, rows, :] = am[j, i] + bm[j, i] * seg_entry + qm[j, i] * seg_after
            return carry

        hours_loop(steps, finish, 0)
        filt_out[:, j * LANES:(j + 1) * LANES] = filt_v[j]
        smooth_out[:, j * LANES:(j + 1) * LANES] = smooth_v[j]

    for copy in list(core_copies.values()) + list(y_copies.values()):
        copy.wait_send()
    for copy in part_copies + early_copies + late_copies:
        copy.wait_send()


def per_device(nt, ns, observations, obs_list, gain_rows, decay, smooth_gain, model_rate, first_state):
    ny = ns // 2
    hours, depth = observations.shape
    modes = gain_rows.shape[1]
    width = modes // ns
    halves = width // LANES
    steps = hours // SEGS
    f32 = jnp.float32
    dma = pltpu.SemaphoreType.DMA
    any_space = pl.BlockSpec(memory_space=pl.ANY)
    tiles = pltpu.VMEM((halves, steps, SEGS, LANES), f32)
    plane = pltpu.VMEM((halves, hours, LANES), f32)
    planes = pltpu.VMEM((ny, halves, hours, LANES), f32)
    group_tiles = pltpu.VMEM((ny, halves, steps, SEGS, LANES), f32)
    params = pltpu.VMEM((modes // LANES, LANES), f32)
    out = pltpu.VMEM((hours, width), f32)
    vmem_space = pl.BlockSpec(memory_space=pltpu.VMEM)
    return pl.pallas_call(
        functools.partial(kernel, nt, ny),
        out_shape=(out, out),
        in_specs=[any_space] * 7,
        out_specs=(vmem_space, vmem_space),
        scratch_shapes=[
            pltpu.VMEM((hours, depth), jnp.bfloat16),
            pltpu.VMEM(obs_list.shape[::-1], jnp.int32),
            pltpu.VMEM((ny * halves, depth, 2 * LANES), jnp.bfloat16),
            planes, planes, params, params,
            planes, planes, planes, planes,
            tiles, group_tiles, tiles, group_tiles, group_tiles, group_tiles, group_tiles, tiles, tiles,
            pltpu.VMEM((nt, halves, 4, LANES), f32),
            pltpu.VMEM((nt, halves, 2, LANES), f32),
            pltpu.VMEM((ny, halves, 2, LANES), f32),
            pltpu.VMEM((ny, halves, 2, LANES), f32),
            plane, plane, pltpu.VMEM((hours, 2 * LANES), f32),
            dma((CHUNKS,)), dma((CHUNKS, 2)), dma((ny * halves, 2)), dma, dma((ny, halves)), dma((ny, halves)), dma((2,)),
            dma((ny, halves)), dma((ny, halves)), dma((ny, halves)), dma((ny, halves)),
            dma((ny,)), dma((ny,)), dma((nt,)), dma((nt,)), dma((nt,)), dma((nt,)),
        ],
        compiler_params=pltpu.CompilerParams(
            collective_id=0, has_side_effects=True, vmem_limit_bytes=56 * 1024 * 1024
        ),
        cost_estimate=pl.CostEstimate(
            flops=2 * hours * depth * modes, bytes_accessed=2 * depth * (hours + modes), transcendentals=0
        ),
    )(
        observations, obs_list.T, gain_rows, decay, smooth_gain,
        model_rate.reshape(modes // LANES, LANES), first_state.reshape(modes // LANES, LANES),
    )


def solution(mesh):
    nt, ns = mesh.shape["tm"], mesh.shape["sensor"]
    in_specs = (
        P("tm", "sensor"),
        P("tm", "sensor"),
        P("sensor", None),
        P("tm", None),
        P("tm", None),
        P(),
        P(),
    )
    out_specs = (P("tm", "sensor"), P("tm", "sensor"))
    return jax.shard_map(
        functools.partial(per_device, nt, ns),
        mesh=mesh, in_specs=in_specs, out_specs=out_specs, check_vma=False,
    )
```

```python
import functools
import jax
import jax.numpy as jnp
from jax import lax
from jax.experimental import pallas as pl
from jax.experimental.pallas import tpu as pltpu
from jax.sharding import PartitionSpec as P

LANES = 128
SEGS = 8
CHUNKS = 4
MESH = pl.DeviceIdType.MESH


def shift_rows(value, count, fill):
    rows = lax.broadcasted_iota(jnp.int32, value.shape, 0)
    moved = pltpu.roll(value, count % SEGS, 0)
    inside = (rows >= count) if count > 0 else (rows < SEGS + count)
    return jnp.where(inside, moved, jnp.float32(fill))


def factor_levels(factor, sign):
    levels = []
    for count in (1, 2, 4):
        levels.append(factor)
        factor = factor * shift_rows(factor, sign * count, 1.0)
    return levels, factor


def chain_rows(levels, value, sign):
    for level, count in zip(levels, (1, 2, 4)):
        value = value + level * shift_rows(value, sign * count, 0.0)
    return value


def kernel(
    nt, ny,
    obs, olist, gain, decay, sgain, rate, first,
    filt_out, smooth_out,
    obs_v, list_v, gain_v, dec_v, sg_v, rate_v, first_v,
    total_v, crecv, acc, yrecv,
    um, fm, am, dm, gm, cm, pm, qm, bm,
    early, late, part_send, part_recv, filt_v, smooth_v,
    obs_sem, gain0_sem, gain_sem, list_sem, dec_sem, sg_sem, par_sem,
    cs_sem, cr_sem, ys_sem, yr_sem, ps_sem, pr_sem, es_sem, er_sem, ls_sem, lr_sem,
):
    tm = lax.axis_index("tm")
    sensor = lax.axis_index("sensor")
    y = sensor // 2
    core = sensor % 2
    partner = sensor + 1 - 2 * core
    hours, depth = obs_v.shape
    halves = acc.shape[1]
    width = halves * LANES
    blocks = depth // LANES
    steps = hours // SEGS
    chunk = depth // CHUNKS
    shifts = list(range(1, ny)) + [0]
    last = ny - 1

    def mine_at(k):
        return lax.rem(y + k, ny) * 2 + core

    def columns(dest, j):
        return pl.ds(pl.multiple_of(dest * width + j * LANES, LANES), LANES)

    def gain_copy(n, rows, sem):
        here = pl.ds(pl.multiple_of(lax.rem(y + shifts[n], ny) * 2 * width, LANES), 2 * width)
        return pltpu.make_async_copy(gain.at[rows, here], gain_v.at[n, rows], sem)

    list_copy = pltpu.make_async_copy(olist, list_v, list_sem)
    list_copy.start()
    obs_copies, gain0_copies = [], []
    for n in range(CHUNKS):
        part = pl.ds(n * chunk, chunk)
        obs_copies.append(pltpu.make_async_copy(obs.at[:, part], obs_v.at[:, part], obs_sem.at[n]))
        gain0_copies.append(gain_copy(0, part, gain0_sem.at[n]))
        obs_copies[-1].start()
        gain0_copies[-1].start()
    everything = pl.ds(0, depth)
    gain_copies = {n: gain_copy(n, everything, gain_sem.at[n]) for n in range(1, ny)}
    steady_copies = []
    for n in range(ny):
        for j in range(halves):
            here = columns(mine_at(shifts[n]), j)
            steady_copies.append(pltpu.make_async_copy(decay.at[:, here], dec_v.at[n, j], dec_sem.at[n, j]))
            steady_copies.append(pltpu.make_async_copy(sgain.at[:, here], sg_v.at[n, j], sg_sem.at[n, j]))
    steady_copies.append(pltpu.make_async_copy(rate, rate_v, par_sem.at[0]))
    steady_copies.append(pltpu.make_async_copy(first, first_v, par_sem.at[1]))

    barrier = pltpu.get_barrier_semaphore()
    peers = [(tm, partner)]
    peers += [(tm, mine_at(k)) for k in range(1, ny)]
    peers += [(lax.rem(tm + k, nt), sensor) for k in range(1, nt)]
    for peer in peers:
        pl.semaphore_signal(barrier, inc=1, device_id=peer, device_id_type=MESH)

    list_copy.wait()
    place = list_v[...] - sensor * blocks
    valid = (place >= 0) & (place < blocks)
    bit = jnp.where(valid, lax.shift_left(jnp.int32(1), jnp.where(valid, place, 0)), 0)
    flat = jnp.broadcast_to(jnp.sum(bit, axis=0, keepdims=True), (LANES, hours))
    bits = jnp.transpose(flat)

    low_bits = (bits & 0xFFFF).astype(jnp.int16)
    high_bits = lax.shift_right_logical(bits, 16).astype(jnp.int16)

    def gated(b):
        part = obs_v[:, b * LANES:(b + 1) * LANES]
        word, place = (low_bits, b) if b < 16 else (high_bits, b - 16)
        flag = jnp.int16((1 << place) if place < 15 else -32768)
        return jnp.where((word & flag) != 0, part, jnp.bfloat16(0))

    total = None
    for n in range(CHUNKS):
        obs_copies[n].wait()
        gain0_copies[n].wait()
        part = pl.ds(n * chunk, chunk)
        per = blocks // CHUNKS
        weighted = jnp.concatenate([gated(b) for b in range(n * per, (n + 1) * per)], axis=1)
        obs_v[:, part] = weighted
        term = jnp.dot(weighted, gain_v[0, part], preferred_element_type=jnp.float32)
        total = term if total is None else total + term
        if n == CHUNKS // 2 - 1:
            for copy in steady_copies + list(gain_copies.values()):
                copy.start()

    core_copies, y_copies = {}, {}

    def hand_over(n, total):
        for side in range(2):
            for j in range(halves):
                at = (side * halves + j) * LANES
                total_v[n, side, j] = total[:, at:at + LANES]
        for j in range(halves):
            copy = pltpu.make_async_remote_copy(
                total_v.at[n, 1 - core, j], crecv.at[n, j], cs_sem.at[n, j], cr_sem.at[n, j],
                device_id=(tm, partner), device_id_type=MESH,
            )
            copy.start()
            core_copies[n, j] = copy

    def product(n):
        return jnp.dot(obs_v[...], gain_v[n], preferred_element_type=jnp.float32)

    def join(n, j):
        core_copies[n, j].wait_recv()
        acc[n, j] = total_v[n, core, j] + crecv[n, j]

    def send_y(n, j):
        join(n, j)
        copy = pltpu.make_async_remote_copy(
            acc.at[n, j], yrecv.at[n, j], ys_sem.at[n, j], yr_sem.at[n, j],
            device_id=(tm, mine_at(shifts[n])), device_id_type=MESH,
        )
        copy.start()
        y_copies[n, j] = copy

    away = [(n, j) for n in range(last) for j in range(halves)]
    home = [(last, j) for j in range(halves)]
    pl.semaphore_wait(barrier, len(peers))
    hand_over(0, total)
    for at in away[:halves]:
        send_y(*at)
    for n in range(1, last):
        gain_copies[n].wait()
        hand_over(n, product(n))
        for j in range(halves):
            send_y(n, j)
    if last > 0:
        gain_copies[last].wait()

    for copy in steady_copies:
        copy.wait()
    row_ids = lax.broadcasted_iota(jnp.int32, (SEGS, LANES), 0)
    if last > 0:
        total = product(last)
    last_row = (row_ids == SEGS - 1) & (tm == nt - 1)
    ones = jnp.ones((SEGS, LANES), jnp.float32)
    zeros = jnp.zeros((SEGS, LANES), jnp.float32)
    rates = {
        (n, j): jnp.broadcast_to(rate_v[pl.ds(mine_at(shifts[n]) * halves + j, 1), :], (SEGS, LANES))
        for n, j in away + home
    }
    prod = {at: ones for at in away + home}
    for i in range(steps):
        for at in away + home:
            d = dec_v[at[0], at[1], pl.ds(i, SEGS, stride=steps), :]
            prod[at] = d * prod[at]
            dm[at[0], at[1], i] = d
            pm[at[0], at[1], i] = prod[at]
    back = {at: ones for at in away + home}
    linear = {at: zeros for at in away + home}
    for i in reversed(range(steps)):
        for at in away + home:
            n, j = at
            g = sg_v[n, j, pl.ds(i, SEGS, stride=steps), :]
            if i == steps - 1:
                g = jnp.where(last_row, 0.0, g)
            c = 1.0 - g * rates[at]
            linear[at] = g * linear[at] + c * pm[n, j, i]
            back[at] = g * back[at]
            gm[n, j, i] = g
            cm[n, j, i] = c
            if n == last:
                qm[j, i] = back[at]
                bm[j, i] = linear[at]
    p_levels, q_levels, p_before, q_after, b_after = {}, {}, {}, {}, {}
    for at in away + home:
        p_levels[at], p_all = factor_levels(prod[at], 1)
        q_levels[at], q_all = factor_levels(back[at], -1)
        p_before[at] = shift_rows(p_all, 1, 1.0)
        q_after[at] = shift_rows(q_all, -1, 1.0)
        if at[0] == last:
            b_all = chain_rows(q_levels[at], linear[at] * p_before[at], -1)
            b_after[at] = shift_rows(b_all, -1, 0.0)
            early[tm, at[1], 0:1] = p_all[SEGS - 1:SEGS]
            early[tm, at[1], 1:2] = q_all[0:1]
            early[tm, at[1], 2:3] = b_all[0:1]
            early[tm, at[1], 3:4] = jnp.zeros((1, LANES), jnp.float32)
    if last > 0:
        hand_over(last, total)

    def summaries(group):
        state = {at: zeros for at in group}
        for i in range(steps):
            for at in group:
                n, j = at
                inflow = acc[n, j, pl.ds(i, SEGS, stride=steps), :]
                if n == last:
                    um[j, i] = inflow
                state[at] = dm[n, j, i] * state[at] + inflow
                fm[n, j, i] = state[at]
        back = {at: zeros for at in group}
        for i in reversed(range(steps)):
            for at in group:
                n, j = at
                back[at] = gm[n, j, i] * back[at] + cm[n, j, i] * fm[n, j, i]
        result = {}
        for at in group:
            f_all = chain_rows(p_levels[at], state[at], 1)
            f_before = shift_rows(f_all, 1, 0.0)
            a_all = chain_rows(q_levels[at], back[at] + linear[at] * f_before, -1)
            result[at] = (f_all[SEGS - 1:SEGS], a_all[0:1])
        return result

    part_copies = []
    away_result = summaries(away)
    for n in range(last):
        for j in range(halves):
            part_send[n, j, 0:1], part_send[n, j, 1:2] = away_result[n, j]
        copy = pltpu.make_async_remote_copy(
            part_send.at[n], part_recv.at[n], ps_sem.at[n], pr_sem.at[n],
            device_id=(tm, mine_at(shifts[n])), device_id_type=MESH,
        )
        copy.start()
        part_copies.append(copy)
    early_copies = []
    for k in range(1, nt):
        copy = pltpu.make_async_remote_copy(
            early.at[tm], early.at[tm], es_sem.at[k], er_sem.at[k],
            device_id=(lax.rem(tm + k, nt), sensor), device_id_type=MESH,
        )
        copy.start()
        early_copies.append(copy)

    for at in home:
        join(*at)
    home_result = summaries(home)
    for copy in part_copies:
        copy.wait_recv()
    for n, j in home:
        f_row, a_row = home_result[n, j]
        for source in range(last):
            f_row = f_row + part_recv[source, j, 0:1]
            a_row = a_row + part_recv[source, j, 1:2]
        late[tm, j, 0:1] = f_row
        late[tm, j, 1:2] = a_row
    late_copies = []
    for k in range(1, nt):
        copy = pltpu.make_async_remote_copy(
            late.at[tm], late.at[tm], ls_sem.at[k], lr_sem.at[k],
            device_id=(lax.rem(tm + k, nt), sensor), device_id_type=MESH,
        )
        copy.start()
        late_copies.append(copy)
    f_before, a_after = {}, {}
    for at in home:
        j = at[1]
        for n in range(last):
            y_copies[n, j].wait_recv()
        state = zeros
        for i in range(steps):
            inflow = um[j, i]
            for n in range(last):
                inflow = inflow + yrecv[n, j, pl.ds(i, SEGS, stride=steps), :]
            state = dm[last, j, i] * state + inflow
            fm[last, j, i] = state
        back = zeros
        for i in reversed(range(steps)):
            back = gm[last, j, i] * back + cm[last, j, i] * fm[last, j, i]
            am[j, i] = back
        f_before[at] = shift_rows(chain_rows(p_levels[at], state, 1), 1, 0.0)
        a_all = chain_rows(q_levels[at], back + linear[at] * f_before[at], -1)
        a_after[at] = shift_rows(a_all, -1, 0.0)

    for copy in early_copies + late_copies:
        copy.wait_recv()
    for at in home:
        j = at[1]
        entry = first_v[pl.ds(sensor * halves + j, 1), :]
        entries, mine = [], entry
        for t in range(nt):
            mine = jnp.where(tm == t, entry, mine)
            entries.append(entry)
            entry = early[t, j, 0:1] * entry + late[t, j, 0:1]
        after = jnp.zeros((1, LANES), jnp.float32)
        mine_after = after
        for t in reversed(range(nt)):
            mine_after = jnp.where(tm == t, after, mine_after)
            after = early[t, j, 1:2] * after + (late[t, j, 1:2] + early[t, j, 2:3] * entries[t])
        seg_entry = p_before[at] * mine + f_before[at]
        seg_after = q_after[at] * mine_after + (a_after[at] + b_after[at] * mine)
        for i in range(steps):
            rows = pl.ds(i, SEGS, stride=steps)
            filt_v[j, rows, :] = fm[last, j, i] + pm[last, j, i] * seg_entry
            smooth_v[j, rows, :] = am[j, i] + bm[j, i] * seg_entry + qm[j, i] * seg_after
        filt_out[:, j * LANES:(j + 1) * LANES] = filt_v[j]
        smooth_out[:, j * LANES:(j + 1) * LANES] = smooth_v[j]

    for copy in list(core_copies.values()) + list(y_copies.values()):
        copy.wait_send()
    for copy in part_copies + early_copies + late_copies:
        copy.wait_send()


def per_device(nt, ns, observations, obs_list, gain_rows, decay, smooth_gain, model_rate, first_state):
    ny = ns // 2
    hours, depth = observations.shape
    modes = gain_rows.shape[1]
    width = modes // ns
    halves = width // LANES
    steps = hours // SEGS
    f32 = jnp.float32
    dma = pltpu.SemaphoreType.DMA
    any_space = pl.BlockSpec(memory_space=pl.ANY)
    tiles = pltpu.VMEM((halves, steps, SEGS, LANES), f32)
    plane = pltpu.VMEM((halves, hours, LANES), f32)
    planes = pltpu.VMEM((ny, halves, hours, LANES), f32)
    group_tiles = pltpu.VMEM((ny, halves, steps, SEGS, LANES), f32)
    params = pltpu.VMEM((modes // LANES, LANES), f32)
    out = pltpu.VMEM((hours, width), f32)
    vmem_space = pl.BlockSpec(memory_space=pltpu.VMEM)
    return pl.pallas_call(
        functools.partial(kernel, nt, ny),
        out_shape=(out, out),
        in_specs=[any_space] * 7,
        out_specs=(vmem_space, vmem_space),
        scratch_shapes=[
            pltpu.VMEM((hours, depth), jnp.bfloat16),
            pltpu.VMEM(obs_list.shape[::-1], jnp.int32),
            pltpu.VMEM((ny, depth, 2 * width), jnp.bfloat16),
            planes, planes, params, params,
            pltpu.VMEM((ny, 2, halves, hours, LANES), f32), planes, planes, planes,
            tiles, group_tiles, tiles, group_tiles, group_tiles, group_tiles, group_tiles, tiles, tiles,
            pltpu.VMEM((nt, halves, 4, LANES), f32),
            pltpu.VMEM((nt, halves, 2, LANES), f32),
            pltpu.VMEM((ny, halves, 2, LANES), f32),
            pltpu.VMEM((ny, halves, 2, LANES), f32),
            plane, plane,
            dma((CHUNKS,)), dma((CHUNKS,)), dma((ny,)), dma, dma((ny, halves)), dma((ny, halves)), dma((2,)),
            dma((ny, halves)), dma((ny, halves)), dma((ny, halves)), dma((ny, halves)),
            dma((ny,)), dma((ny,)), dma((nt,)), dma((nt,)), dma((nt,)), dma((nt,)),
        ],
        compiler_params=pltpu.CompilerParams(
            collective_id=0, has_side_effects=True, vmem_limit_bytes=56 * 1024 * 1024
        ),
        cost_estimate=pl.CostEstimate(
            flops=2 * hours * depth * modes, bytes_accessed=2 * depth * (hours + modes), transcendentals=0
        ),
    )(
        observations, obs_list.T, gain_rows, decay, smooth_gain,
        model_rate.reshape(modes // LANES, LANES), first_state.reshape(modes // LANES, LANES),
    )


def solution(mesh):
    nt, ns = mesh.shape["tm"], mesh.shape["sensor"]
    in_specs = (
        P("tm", "sensor"),
        P("tm", "sensor"),
        P("sensor", None),
        P("tm", None),
        P("tm", None),
        P(),
        P(),
    )
    out_specs = (P("tm", "sensor"), P("tm", "sensor"))
    return jax.shard_map(
        functools.partial(per_device, nt, ns),
        mesh=mesh, in_specs=in_specs, out_specs=out_specs, check_vma=False,
    )
```

```python
import functools
import jax
import jax.numpy as jnp
from jax import lax
from jax.experimental import pallas as pl
from jax.experimental.pallas import tpu as pltpu
from jax.sharding import PartitionSpec as P

LANES = 128
SEGS = 8
CHUNKS = 4
PIECES = 4
MESH = pl.DeviceIdType.MESH


def shift_rows(value, count, fill):
    rows = lax.broadcasted_iota(jnp.int32, value.shape, 0)
    moved = pltpu.roll(value, count % SEGS, 0)
    inside = (rows >= count) if count > 0 else (rows < SEGS + count)
    return jnp.where(inside, moved, jnp.float32(fill))


def factor_levels(factor, sign):
    levels = []
    for count in (1, 2, 4):
        levels.append(factor)
        factor = factor * shift_rows(factor, sign * count, 1.0)
    return levels, factor


def chain_rows(levels, value, sign):
    for level, count in zip(levels, (1, 2, 4)):
        value = value + level * shift_rows(value, sign * count, 0.0)
    return value


def kernel(
    nt, ny,
    obs, olist, gain, decay, sgain, rate, first,
    filt_out, smooth_out,
    obs_v, list_v, gain_v, dec_v, sg_v, rate_v, first_v,
    total_v, crecv, acc, yrecv,
    um, fm, am, dm, gm, cm, pm, qm, bm,
    early, late, part_send, part_recv, filt_v, smooth_v,
    obs_sem, gain0_sem, gain_sem, list_sem, dec_sem, sg_sem, par_sem,
    cs_sem, cr_sem, ys_sem, yr_sem, ps_sem, pr_sem, es_sem, er_sem, ls_sem, lr_sem,
):
    tm = lax.axis_index("tm")
    sensor = lax.axis_index("sensor")
    y = sensor // 2
    core = sensor % 2
    partner = sensor + 1 - 2 * core
    hours, depth = obs_v.shape
    halves = acc.shape[1]
    width = halves * LANES
    blocks = depth // LANES
    steps = hours // SEGS
    chunk = depth // CHUNKS
    shifts = list(range(1, ny)) + [0]
    last = ny - 1

    def mine_at(k):
        return lax.rem(y + k, ny) * 2 + core

    def columns(dest, j):
        return pl.ds(pl.multiple_of(dest * width + j * LANES, LANES), LANES)

    def gain_copy(n, rows, sem):
        here = pl.ds(pl.multiple_of(lax.rem(y + shifts[n], ny) * 2 * width, LANES), 2 * width)
        return pltpu.make_async_copy(gain.at[rows, here], gain_v.at[n, rows], sem)

    list_copy = pltpu.make_async_copy(olist, list_v, list_sem)
    list_copy.start()
    obs_copies, gain0_copies = [], []
    for n in range(CHUNKS):
        part = pl.ds(n * chunk, chunk)
        obs_copies.append(pltpu.make_async_copy(obs.at[:, part], obs_v.at[:, part], obs_sem.at[n]))
        gain0_copies.append(gain_copy(0, part, gain0_sem.at[n]))
        obs_copies[-1].start()
        gain0_copies[-1].start()
    everything = pl.ds(0, depth)
    gain_copies = {n: gain_copy(n, everything, gain_sem.at[n]) for n in range(1, ny)}
    steady_copies = []
    for n in range(ny):
        for j in range(halves):
            here = columns(mine_at(shifts[n]), j)
            steady_copies.append(pltpu.make_async_copy(decay.at[:, here], dec_v.at[n, j], dec_sem.at[n, j]))
            steady_copies.append(pltpu.make_async_copy(sgain.at[:, here], sg_v.at[n, j], sg_sem.at[n, j]))
    steady_copies.append(pltpu.make_async_copy(rate, rate_v, par_sem.at[0]))
    steady_copies.append(pltpu.make_async_copy(first, first_v, par_sem.at[1]))

    barrier = pltpu.get_barrier_semaphore()
    peers = [(tm, partner)]
    peers += [(tm, mine_at(k)) for k in range(1, ny)]
    peers += [(lax.rem(tm + k, nt), sensor) for k in range(1, nt)]
    for peer in peers:
        pl.semaphore_signal(barrier, inc=1, device_id=peer, device_id_type=MESH)

    list_copy.wait()
    place = list_v[...] - sensor * blocks
    valid = (place >= 0) & (place < blocks)
    bit = jnp.where(valid, lax.shift_left(jnp.int32(1), jnp.where(valid, place, 0)), 0)
    flat = jnp.broadcast_to(jnp.sum(bit, axis=0, keepdims=True), (LANES, hours))
    bits = jnp.transpose(flat)

    low_bits = (bits & 0xFFFF).astype(jnp.int16)
    high_bits = lax.shift_right_logical(bits, 16).astype(jnp.int16)

    def gated(b):
        part = obs_v[:, b * LANES:(b + 1) * LANES]
        word, place = (low_bits, b) if b < 16 else (high_bits, b - 16)
        flag = jnp.int16((1 << place) if place < 15 else -32768)
        return jnp.where((word & flag) != 0, part, jnp.bfloat16(0))

    total = None
    for n in range(CHUNKS):
        obs_copies[n].wait()
        gain0_copies[n].wait()
        part = pl.ds(n * chunk, chunk)
        per = blocks // CHUNKS
        weighted = jnp.concatenate([gated(b) for b in range(n * per, (n + 1) * per)], axis=1)
        obs_v[:, part] = weighted
        term = jnp.dot(weighted, gain_v[0, part], preferred_element_type=jnp.float32)
        total = term if total is None else total + term
        if n == CHUNKS // 2 - 1:
            for copy in steady_copies + list(gain_copies.values()):
                copy.start()

    core_copies, y_copies = {}, {}

    def hand_over(n, total):
        for side in range(2):
            for j in range(halves):
                at = (side * halves + j) * LANES
                total_v[n, side, j] = total[:, at:at + LANES]
        for j in range(halves):
            copy = pltpu.make_async_remote_copy(
                total_v.at[n, 1 - core, j], crecv.at[n, j], cs_sem.at[n, j], cr_sem.at[n, j],
                device_id=(tm, partner), device_id_type=MESH,
            )
            copy.start()
            core_copies[n, j] = copy

    def product(n):
        return jnp.dot(obs_v[...], gain_v[n], preferred_element_type=jnp.float32)

    def join(n, j):
        core_copies[n, j].wait_recv()
        acc[n, j] = total_v[n, core, j] + crecv[n, j]

    def send_y(n, j):
        join(n, j)
        y_copies[n, j] = []
        for piece in range(PIECES):
            rows = pl.ds(piece * (hours // PIECES), hours // PIECES)
            copy = pltpu.make_async_remote_copy(
                acc.at[n, j, rows], yrecv.at[n, j, rows],
                ys_sem.at[n, j, piece], yr_sem.at[n, j, piece],
                device_id=(tm, mine_at(shifts[n])), device_id_type=MESH,
            )
            copy.start()
            y_copies[n, j].append(copy)

    away = [(n, j) for n in range(last) for j in range(halves)]
    home = [(last, j) for j in range(halves)]
    pl.semaphore_wait(barrier, len(peers))
    hand_over(0, total)
    for at in away[:halves]:
        send_y(*at)
    for n in range(1, last):
        gain_copies[n].wait()
        hand_over(n, product(n))
        for j in range(halves):
            send_y(n, j)
    if last > 0:
        gain_copies[last].wait()

    for copy in steady_copies:
        copy.wait()
    row_ids = lax.broadcasted_iota(jnp.int32, (SEGS, LANES), 0)
    if last > 0:
        total = product(last)
    last_row = (row_ids == SEGS - 1) & (tm == nt - 1)
    ones = jnp.ones((SEGS, LANES), jnp.float32)
    zeros = jnp.zeros((SEGS, LANES), jnp.float32)
    rates = {
        (n, j): jnp.broadcast_to(rate_v[pl.ds(mine_at(shifts[n]) * halves + j, 1), :], (SEGS, LANES))
        for n, j in away + home
    }
    prod = {at: ones for at in away + home}
    for i in range(steps):
        for at in away + home:
            d = dec_v[at[0], at[1], pl.ds(i, SEGS, stride=steps), :]
            prod[at] = d * prod[at]
            dm[at[0], at[1], i] = d
            pm[at[0], at[1], i] = prod[at]
    back = {at: ones for at in away + home}
    linear = {at: zeros for at in away + home}
    for i in reversed(range(steps)):
        for at in away + home:
            n, j = at
            g = sg_v[n, j, pl.ds(i, SEGS, stride=steps), :]
            if i == steps - 1:
                g = jnp.where(last_row, 0.0, g)
            c = 1.0 - g * rates[at]
            linear[at] = g * linear[at] + c * pm[n, j, i]
            back[at] = g * back[at]
            gm[n, j, i] = g
            cm[n, j, i] = c
            if n == last:
                qm[j, i] = back[at]
                bm[j, i] = linear[at]
    p_levels, q_levels, p_before, q_after, b_after = {}, {}, {}, {}, {}
    for at in away + home:
        p_levels[at], p_all = factor_levels(prod[at], 1)
        q_levels[at], q_all = factor_levels(back[at], -1)
        p_before[at] = shift_rows(p_all, 1, 1.0)
        q_after[at] = shift_rows(q_all, -1, 1.0)
        if at[0] == last:
            b_all = chain_rows(q_levels[at], linear[at] * p_before[at], -1)
            b_after[at] = shift_rows(b_all, -1, 0.0)
            early[tm, at[1], 0:1] = p_all[SEGS - 1:SEGS]
            early[tm, at[1], 1:2] = q_all[0:1]
            early[tm, at[1], 2:3] = b_all[0:1]
            early[tm, at[1], 3:4] = jnp.zeros((1, LANES), jnp.float32)
    if last > 0:
        hand_over(last, total)

    def summaries(group):
        state = {at: zeros for at in group}
        for i in range(steps):
            for at in group:
                n, j = at
                inflow = acc[n, j, pl.ds(i, SEGS, stride=steps), :]
                if n == last:
                    um[j, i] = inflow
                state[at] = dm[n, j, i] * state[at] + inflow
                fm[n, j, i] = state[at]
        back = {at: zeros for at in group}
        for i in reversed(range(steps)):
            for at in group:
                n, j = at
                back[at] = gm[n, j, i] * back[at] + cm[n, j, i] * fm[n, j, i]
        result = {}
        for at in group:
            f_all = chain_rows(p_levels[at], state[at], 1)
            f_before = shift_rows(f_all, 1, 0.0)
            a_all = chain_rows(q_levels[at], back[at] + linear[at] * f_before, -1)
            result[at] = (f_all[SEGS - 1:SEGS], a_all[0:1])
        return result

    part_copies = []
    away_result = summaries(away)
    for n in range(last):
        for j in range(halves):
            part_send[n, j, 0:1], part_send[n, j, 1:2] = away_result[n, j]
        copy = pltpu.make_async_remote_copy(
            part_send.at[n], part_recv.at[n], ps_sem.at[n], pr_sem.at[n],
            device_id=(tm, mine_at(shifts[n])), device_id_type=MESH,
        )
        copy.start()
        part_copies.append(copy)
    early_copies = []
    for k in range(1, nt):
        copy = pltpu.make_async_remote_copy(
            early.at[tm], early.at[tm], es_sem.at[k], er_sem.at[k],
            device_id=(lax.rem(tm + k, nt), sensor), device_id_type=MESH,
        )
        copy.start()
        early_copies.append(copy)

    for at in home:
        join(*at)
    home_result = summaries(home)
    for copy in part_copies:
        copy.wait_recv()
    for n, j in home:
        f_row, a_row = home_result[n, j]
        for source in range(last):
            f_row = f_row + part_recv[source, j, 0:1]
            a_row = a_row + part_recv[source, j, 1:2]
        late[tm, j, 0:1] = f_row
        late[tm, j, 1:2] = a_row
    late_copies = []
    for k in range(1, nt):
        copy = pltpu.make_async_remote_copy(
            late.at[tm], late.at[tm], ls_sem.at[k], lr_sem.at[k],
            device_id=(lax.rem(tm + k, nt), sensor), device_id_type=MESH,
        )
        copy.start()
        late_copies.append(copy)
    for pieces in y_copies.values():
        for copy in pieces:
            copy.wait_recv()
    state = {at: zeros for at in home}
    for i in range(steps):
        for at in home:
            j = at[1]
            inflow = um[j, i]
            for n in range(last):
                inflow = inflow + yrecv[n, j, pl.ds(i, SEGS, stride=steps), :]
            state[at] = dm[last, j, i] * state[at] + inflow
            fm[last, j, i] = state[at]
    back = {at: zeros for at in home}
    for i in reversed(range(steps)):
        for at in home:
            j = at[1]
            back[at] = gm[last, j, i] * back[at] + cm[last, j, i] * fm[last, j, i]
            am[j, i] = back[at]
    f_before, a_after = {}, {}
    for at in home:
        f_before[at] = shift_rows(chain_rows(p_levels[at], state[at], 1), 1, 0.0)
        a_all = chain_rows(q_levels[at], back[at] + linear[at] * f_before[at], -1)
        a_after[at] = shift_rows(a_all, -1, 0.0)

    for copy in early_copies + late_copies:
        copy.wait_recv()
    for at in home:
        j = at[1]
        entry = first_v[pl.ds(sensor * halves + j, 1), :]
        entries, mine = [], entry
        for t in range(nt):
            mine = jnp.where(tm == t, entry, mine)
            entries.append(entry)
            entry = early[t, j, 0:1] * entry + late[t, j, 0:1]
        after = jnp.zeros((1, LANES), jnp.float32)
        mine_after = after
        for t in reversed(range(nt)):
            mine_after = jnp.where(tm == t, after, mine_after)
            after = early[t, j, 1:2] * after + (late[t, j, 1:2] + early[t, j, 2:3] * entries[t])
        seg_entry = p_before[at] * mine + f_before[at]
        seg_after = q_after[at] * mine_after + (a_after[at] + b_after[at] * mine)
        for i in range(steps):
            rows = pl.ds(i, SEGS, stride=steps)
            filt_v[j, rows, :] = fm[last, j, i] + pm[last, j, i] * seg_entry
            smooth_v[j, rows, :] = am[j, i] + bm[j, i] * seg_entry + qm[j, i] * seg_after
        filt_out[:, j * LANES:(j + 1) * LANES] = filt_v[j]
        smooth_out[:, j * LANES:(j + 1) * LANES] = smooth_v[j]

    for copy in list(core_copies.values()) + sum(y_copies.values(), []):
        copy.wait_send()
    for copy in part_copies + early_copies + late_copies:
        copy.wait_send()


def per_device(nt, ns, observations, obs_list, gain_rows, decay, smooth_gain, model_rate, first_state):
    ny = ns // 2
    hours, depth = observations.shape
    modes = gain_rows.shape[1]
    width = modes // ns
    halves = width // LANES
    steps = hours // SEGS
    f32 = jnp.float32
    dma = pltpu.SemaphoreType.DMA
    any_space = pl.BlockSpec(memory_space=pl.ANY)
    tiles = pltpu.VMEM((halves, steps, SEGS, LANES), f32)
    plane = pltpu.VMEM((halves, hours, LANES), f32)
    planes = pltpu.VMEM((ny, halves, hours, LANES), f32)
    group_tiles = pltpu.VMEM((ny, halves, steps, SEGS, LANES), f32)
    params = pltpu.VMEM((modes // LANES, LANES), f32)
    out = pltpu.VMEM((hours, width), f32)
    vmem_space = pl.BlockSpec(memory_space=pltpu.VMEM)
    return pl.pallas_call(
        functools.partial(kernel, nt, ny),
        out_shape=(out, out),
        in_specs=[any_space] * 7,
        out_specs=(vmem_space, vmem_space),
        scratch_shapes=[
            pltpu.VMEM((hours, depth), jnp.bfloat16),
            pltpu.VMEM(obs_list.shape[::-1], jnp.int32),
            pltpu.VMEM((ny, depth, 2 * width), jnp.bfloat16),
            planes, planes, params, params,
            pltpu.VMEM((ny, 2, halves, hours, LANES), f32), planes, planes, planes,
            tiles, group_tiles, tiles, group_tiles, group_tiles, group_tiles, group_tiles, tiles, tiles,
            pltpu.VMEM((nt, halves, 4, LANES), f32),
            pltpu.VMEM((nt, halves, 2, LANES), f32),
            pltpu.VMEM((ny, halves, 2, LANES), f32),
            pltpu.VMEM((ny, halves, 2, LANES), f32),
            plane, plane,
            dma((CHUNKS,)), dma((CHUNKS,)), dma((ny,)), dma, dma((ny, halves)), dma((ny, halves)), dma((2,)),
            dma((ny, halves)), dma((ny, halves)), dma((ny, halves, PIECES)), dma((ny, halves, PIECES)),
            dma((ny,)), dma((ny,)), dma((nt,)), dma((nt,)), dma((nt,)), dma((nt,)),
        ],
        compiler_params=pltpu.CompilerParams(
            collective_id=0, has_side_effects=True, vmem_limit_bytes=56 * 1024 * 1024
        ),
        cost_estimate=pl.CostEstimate(
            flops=2 * hours * depth * modes, bytes_accessed=2 * depth * (hours + modes), transcendentals=0
        ),
    )(
        observations, obs_list.T, gain_rows, decay, smooth_gain,
        model_rate.reshape(modes // LANES, LANES), first_state.reshape(modes // LANES, LANES),
    )


def solution(mesh):
    nt, ns = mesh.shape["tm"], mesh.shape["sensor"]
    in_specs = (
        P("tm", "sensor"),
        P("tm", "sensor"),
        P("sensor", None),
        P("tm", None),
        P("tm", None),
        P(),
        P(),
    )
    out_specs = (P("tm", "sensor"), P("tm", "sensor"))
    return jax.shard_map(
        functools.partial(per_device, nt, ns),
        mesh=mesh, in_specs=in_specs, out_specs=out_specs, check_vma=False,
    )
```

```python
import functools
import jax
import jax.numpy as jnp
from jax import lax
from jax.experimental import pallas as pl
from jax.experimental.pallas import tpu as pltpu
from jax.sharding import PartitionSpec as P

LANES = 128
SEGS = 8
CHUNKS = 4
MESH = pl.DeviceIdType.MESH


def shift_rows(value, count, fill):
    rows = lax.broadcasted_iota(jnp.int32, value.shape, 0)
    moved = pltpu.roll(value, count % SEGS, 0)
    inside = (rows >= count) if count > 0 else (rows < SEGS + count)
    return jnp.where(inside, moved, jnp.float32(fill))


def factor_levels(factor, sign):
    levels = []
    for count in (1, 2, 4):
        levels.append(factor)
        factor = factor * shift_rows(factor, sign * count, 1.0)
    return levels, factor


def chain_rows(levels, value, sign):
    for level, count in zip(levels, (1, 2, 4)):
        value = value + level * shift_rows(value, sign * count, 0.0)
    return value


def kernel(
    nt, ny,
    obs, olist, gain, decay, sgain, rate, first,
    filt_out, smooth_out,
    obs_v, list_v, gain_v, dec_v, sg_v, rate_v, first_v,
    total_v, crecv, acc, yrecv,
    fm, am, dm, gm, cm, pm, qm, bm,
    early, late, filt_v, smooth_v,
    obs_sem, gain0_sem, gain_sem, list_sem, dec_sem, sg_sem, par_sem,
    cs_sem, cr_sem, ys_sem, yr_sem, es_sem, er_sem, ls_sem, lr_sem,
):
    tm = lax.axis_index("tm")
    sensor = lax.axis_index("sensor")
    y = sensor // 2
    core = sensor % 2
    partner = sensor + 1 - 2 * core
    hours, depth = obs_v.shape
    halves = acc.shape[1]
    width = halves * LANES
    blocks = depth // LANES
    steps = hours // SEGS
    chunk = depth // CHUNKS
    shifts = list(range(1, ny)) + [0]
    last = ny - 1

    def mine_at(k):
        return lax.rem(y + k, ny) * 2 + core

    def columns(dest, j):
        return pl.ds(pl.multiple_of(dest * width + j * LANES, LANES), LANES)

    def gain_copy(n, rows, sem):
        here = pl.ds(pl.multiple_of(lax.rem(y + shifts[n], ny) * 2 * width, LANES), 2 * width)
        return pltpu.make_async_copy(gain.at[rows, here], gain_v.at[n, rows], sem)

    list_copy = pltpu.make_async_copy(olist, list_v, list_sem)
    list_copy.start()
    obs_copies, gain0_copies = [], []
    for n in range(CHUNKS):
        part = pl.ds(n * chunk, chunk)
        obs_copies.append(pltpu.make_async_copy(obs.at[:, part], obs_v.at[:, part], obs_sem.at[n]))
        gain0_copies.append(gain_copy(0, part, gain0_sem.at[n]))
        obs_copies[-1].start()
        gain0_copies[-1].start()
    everything = pl.ds(0, depth)
    gain_copies = {n: gain_copy(n, everything, gain_sem.at[n]) for n in range(1, ny)}
    steady_copies = []
    for n in (last,):
        for j in range(halves):
            here = columns(mine_at(shifts[n]), j)
            steady_copies.append(pltpu.make_async_copy(decay.at[:, here], dec_v.at[n, j], dec_sem.at[n, j]))
            steady_copies.append(pltpu.make_async_copy(sgain.at[:, here], sg_v.at[n, j], sg_sem.at[n, j]))
    steady_copies.append(pltpu.make_async_copy(rate, rate_v, par_sem.at[0]))
    steady_copies.append(pltpu.make_async_copy(first, first_v, par_sem.at[1]))

    barrier = pltpu.get_barrier_semaphore()
    peers = [(tm, partner)]
    peers += [(tm, mine_at(k)) for k in range(1, ny)]
    peers += [(lax.rem(tm + k, nt), sensor) for k in range(1, nt)]
    for peer in peers:
        pl.semaphore_signal(barrier, inc=1, device_id=peer, device_id_type=MESH)

    list_copy.wait()
    place = list_v[...] - sensor * blocks
    valid = (place >= 0) & (place < blocks)
    bit = jnp.where(valid, lax.shift_left(jnp.int32(1), jnp.where(valid, place, 0)), 0)
    flat = jnp.broadcast_to(jnp.sum(bit, axis=0, keepdims=True), (LANES, hours))
    bits = jnp.transpose(flat)

    low_bits = (bits & 0xFFFF).astype(jnp.int16)
    high_bits = lax.shift_right_logical(bits, 16).astype(jnp.int16)

    def gated(b):
        part = obs_v[:, b * LANES:(b + 1) * LANES]
        word, place = (low_bits, b) if b < 16 else (high_bits, b - 16)
        flag = jnp.int16((1 << place) if place < 15 else -32768)
        return jnp.where((word & flag) != 0, part, jnp.bfloat16(0))

    total = None
    for n in range(CHUNKS):
        obs_copies[n].wait()
        gain0_copies[n].wait()
        part = pl.ds(n * chunk, chunk)
        per = blocks // CHUNKS
        weighted = jnp.concatenate([gated(b) for b in range(n * per, (n + 1) * per)], axis=1)
        obs_v[:, part] = weighted
        term = jnp.dot(weighted, gain_v[0, part], preferred_element_type=jnp.float32)
        total = term if total is None else total + term
        if n == CHUNKS // 2 - 1:
            for copy in steady_copies + list(gain_copies.values()):
                copy.start()

    core_copies, y_copies = {}, {}

    def hand_over(n, total):
        for side in range(2):
            for j in range(halves):
                at = (side * halves + j) * LANES
                total_v[n, side, j] = total[:, at:at + LANES]
        for j in range(halves):
            copy = pltpu.make_async_remote_copy(
                total_v.at[n, 1 - core, j], crecv.at[n, j], cs_sem.at[n, j], cr_sem.at[n, j],
                device_id=(tm, partner), device_id_type=MESH,
            )
            copy.start()
            core_copies[n, j] = copy

    def product(n):
        return jnp.dot(obs_v[...], gain_v[n], preferred_element_type=jnp.float32)

    def join(n, j):
        core_copies[n, j].wait_recv()
        acc[n, j] = total_v[n, core, j] + crecv[n, j]

    def send_y(n, j):
        join(n, j)
        copy = pltpu.make_async_remote_copy(
            acc.at[n, j], yrecv.at[n, j], ys_sem.at[n, j], yr_sem.at[n, j],
            device_id=(tm, mine_at(shifts[n])), device_id_type=MESH,
        )
        copy.start()
        y_copies[n, j] = copy

    away = [(n, j) for n in range(last) for j in range(halves)]
    home = [(last, j) for j in range(halves)]
    pl.semaphore_wait(barrier, len(peers))
    hand_over(0, total)
    for at in away[:halves]:
        send_y(*at)
    for n in range(1, last):
        gain_copies[n].wait()
        hand_over(n, product(n))
        for j in range(halves):
            send_y(n, j)
    if last > 0:
        gain_copies[last].wait()

    for copy in steady_copies:
        copy.wait()
    row_ids = lax.broadcasted_iota(jnp.int32, (SEGS, LANES), 0)
    if last > 0:
        total = product(last)
    last_row = (row_ids == SEGS - 1) & (tm == nt - 1)
    ones = jnp.ones((SEGS, LANES), jnp.float32)
    zeros = jnp.zeros((SEGS, LANES), jnp.float32)
    rates = {
        (n, j): jnp.broadcast_to(rate_v[pl.ds(mine_at(shifts[n]) * halves + j, 1), :], (SEGS, LANES))
        for n, j in home
    }
    prod = {at: ones for at in home}
    for i in range(steps):
        for at in home:
            d = dec_v[at[0], at[1], pl.ds(i, SEGS, stride=steps), :]
            prod[at] = d * prod[at]
            dm[at[0], at[1], i] = d
            pm[at[0], at[1], i] = prod[at]
    back = {at: ones for at in home}
    linear = {at: zeros for at in home}
    for i in reversed(range(steps)):
        for at in home:
            n, j = at
            g = sg_v[n, j, pl.ds(i, SEGS, stride=steps), :]
            if i == steps - 1:
                g = jnp.where(last_row, 0.0, g)
            c = 1.0 - g * rates[at]
            linear[at] = g * linear[at] + c * pm[n, j, i]
            back[at] = g * back[at]
            gm[n, j, i] = g
            cm[n, j, i] = c
            if n == last:
                qm[j, i] = back[at]
                bm[j, i] = linear[at]
    p_levels, q_levels, p_before, q_after, b_after = {}, {}, {}, {}, {}
    for at in home:
        p_levels[at], p_all = factor_levels(prod[at], 1)
        q_levels[at], q_all = factor_levels(back[at], -1)
        p_before[at] = shift_rows(p_all, 1, 1.0)
        q_after[at] = shift_rows(q_all, -1, 1.0)
        if at[0] == last:
            b_all = chain_rows(q_levels[at], linear[at] * p_before[at], -1)
            b_after[at] = shift_rows(b_all, -1, 0.0)
            early[tm, at[1], 0:1] = p_all[SEGS - 1:SEGS]
            early[tm, at[1], 1:2] = q_all[0:1]
            early[tm, at[1], 2:3] = b_all[0:1]
            early[tm, at[1], 3:4] = jnp.zeros((1, LANES), jnp.float32)
    if last > 0:
        hand_over(last, total)

    early_copies = []
    for k in range(1, nt):
        copy = pltpu.make_async_remote_copy(
            early.at[tm], early.at[tm], es_sem.at[k], er_sem.at[k],
            device_id=(lax.rem(tm + k, nt), sensor), device_id_type=MESH,
        )
        copy.start()
        early_copies.append(copy)

    for at in home:
        join(*at)
    late_copies = []
    f_before, a_after = {}, {}
    for at in home:
        j = at[1]
        for n in range(last):
            y_copies[n, j].wait_recv()
        state = zeros
        for i in range(steps):
            inflow = acc[last, j, pl.ds(i, SEGS, stride=steps), :]
            for n in range(last):
                inflow = inflow + yrecv[n, j, pl.ds(i, SEGS, stride=steps), :]
            state = dm[last, j, i] * state + inflow
            fm[last, j, i] = state
        back = zeros
        for i in reversed(range(steps)):
            back = gm[last, j, i] * back + cm[last, j, i] * fm[last, j, i]
            am[j, i] = back
        f_all = chain_rows(p_levels[at], state, 1)
        f_before[at] = shift_rows(f_all, 1, 0.0)
        a_all = chain_rows(q_levels[at], back + linear[at] * f_before[at], -1)
        a_after[at] = shift_rows(a_all, -1, 0.0)
        late[tm, j, 0:1] = f_all[SEGS - 1:SEGS]
        late[tm, j, 1:2] = a_all[0:1]
        for k in range(1, nt):
            copy = pltpu.make_async_remote_copy(
                late.at[tm, j], late.at[tm, j], ls_sem.at[j, k], lr_sem.at[j, k],
                device_id=(lax.rem(tm + k, nt), sensor), device_id_type=MESH,
            )
            copy.start()
            late_copies.append(copy)

    for copy in early_copies:
        copy.wait_recv()
    for at in home:
        j = at[1]
        for copy in late_copies[j * (nt - 1):(j + 1) * (nt - 1)]:
            copy.wait_recv()
        entry = first_v[pl.ds(sensor * halves + j, 1), :]
        entries, mine = [], entry
        for t in range(nt):
            mine = jnp.where(tm == t, entry, mine)
            entries.append(entry)
            entry = early[t, j, 0:1] * entry + late[t, j, 0:1]
        after = jnp.zeros((1, LANES), jnp.float32)
        mine_after = after
        for t in reversed(range(nt)):
            mine_after = jnp.where(tm == t, after, mine_after)
            after = early[t, j, 1:2] * after + (late[t, j, 1:2] + early[t, j, 2:3] * entries[t])
        seg_entry = p_before[at] * mine + f_before[at]
        seg_after = q_after[at] * mine_after + (a_after[at] + b_after[at] * mine)
        for i in range(steps):
            rows = pl.ds(i, SEGS, stride=steps)
            filt_v[j, rows, :] = fm[last, j, i] + pm[last, j, i] * seg_entry
            smooth_v[j, rows, :] = am[j, i] + bm[j, i] * seg_entry + qm[j, i] * seg_after
        filt_out[:, j * LANES:(j + 1) * LANES] = filt_v[j]
        smooth_out[:, j * LANES:(j + 1) * LANES] = smooth_v[j]

    for copy in list(core_copies.values()) + list(y_copies.values()):
        copy.wait_send()
    for copy in early_copies + late_copies:
        copy.wait_send()


def per_device(nt, ns, observations, obs_list, gain_rows, decay, smooth_gain, model_rate, first_state):
    ny = ns // 2
    hours, depth = observations.shape
    modes = gain_rows.shape[1]
    width = modes // ns
    halves = width // LANES
    steps = hours // SEGS
    f32 = jnp.float32
    dma = pltpu.SemaphoreType.DMA
    any_space = pl.BlockSpec(memory_space=pl.ANY)
    tiles = pltpu.VMEM((halves, steps, SEGS, LANES), f32)
    plane = pltpu.VMEM((halves, hours, LANES), f32)
    planes = pltpu.VMEM((ny, halves, hours, LANES), f32)
    group_tiles = pltpu.VMEM((ny, halves, steps, SEGS, LANES), f32)
    params = pltpu.VMEM((modes // LANES, LANES), f32)
    out = pltpu.VMEM((hours, width), f32)
    vmem_space = pl.BlockSpec(memory_space=pltpu.VMEM)
    return pl.pallas_call(
        functools.partial(kernel, nt, ny),
        out_shape=(out, out),
        in_specs=[any_space] * 7,
        out_specs=(vmem_space, vmem_space),
        scratch_shapes=[
            pltpu.VMEM((hours, depth), jnp.bfloat16),
            pltpu.VMEM(obs_list.shape[::-1], jnp.int32),
            pltpu.VMEM((ny, depth, 2 * width), jnp.bfloat16),
            planes, planes, params, params,
            pltpu.VMEM((ny, 2, halves, hours, LANES), f32), planes, planes, planes,
            group_tiles, tiles, group_tiles, group_tiles, group_tiles, group_tiles, tiles, tiles,
            pltpu.VMEM((nt, halves, 4, LANES), f32),
            pltpu.VMEM((nt, halves, 2, LANES), f32),
            plane, plane,
            dma((CHUNKS,)), dma((CHUNKS,)), dma((ny,)), dma, dma((ny, halves)), dma((ny, halves)), dma((2,)),
            dma((ny, halves)), dma((ny, halves)), dma((ny, halves)), dma((ny, halves)),
            dma((nt,)), dma((nt,)), dma((halves, nt)), dma((halves, nt)),
        ],
        compiler_params=pltpu.CompilerParams(
            collective_id=0, has_side_effects=True, vmem_limit_bytes=56 * 1024 * 1024
        ),
        cost_estimate=pl.CostEstimate(
            flops=2 * hours * depth * modes, bytes_accessed=2 * depth * (hours + modes), transcendentals=0
        ),
    )(
        observations, obs_list.T, gain_rows, decay, smooth_gain,
        model_rate.reshape(modes // LANES, LANES), first_state.reshape(modes // LANES, LANES),
    )


def solution(mesh):
    nt, ns = mesh.shape["tm"], mesh.shape["sensor"]
    in_specs = (
        P("tm", "sensor"),
        P("tm", "sensor"),
        P("sensor", None),
        P("tm", None),
        P("tm", None),
        P(),
        P(),
    )
    out_specs = (P("tm", "sensor"), P("tm", "sensor"))
    return jax.shard_map(
        functools.partial(per_device, nt, ns),
        mesh=mesh, in_specs=in_specs, out_specs=out_specs, check_vma=False,
    )
```
